128 devices in a mesh: clip: 32 (over x, z, core), tm: 4 (over y).
Axes of the slice: x: 4, y: 4, z: 4, core: 2. Of those that a mesh axis runs over, the one named last changes fastest.
Arguments:
- tiles: bfloat16 [1024, 16, 8, 8, 128], P('clip', 'tm'), may hold values from -6 to 6
- buckets: int32 [1024, 1], P('clip'), may hold values from 0 to 31; in each aligned block of 32 rows (0 to 31, 32 to 63, ...) at most 2 rows name the same one
- tile_frames: int32 [1024], P('clip'), may hold values from 4 to 16, as said below
- norm_gain: float32 [128], replicated, may hold values from 0.5 to 1.5
- norm_shift: float32 [128], replicated, may hold values from -3 to 3
- conv_weight: bfloat16 [3, 3, 3, 128, 128], replicated, may hold values from -0.109375 to 0.109375
- conv_bias: float32 [128], replicated, may hold values from -2 to 2
Outputs:
- latents: bfloat16 [2048, 16, 8, 8, 128], P('clip', 'tm')
The draws below stay inside these ranges and needn't reach their ends.
Inputs may be any that keep to these rules, and one draw needn't show every extreme that they name: `buckets`: among the 32 tiles of one reader at most 2 name the same group, and some group gets exactly 2. `tile_frames`: A multiple of 4; the first tile of every reader has all 16 frames.
All inputs are finite; a program needn't handle non-finite values.
Results may differ from the reference program's by a relative error of at most 0.0033.
Values may be sent and summed in bfloat16 or wider, within the bound.
A program may use at most 384 MiB of HBM per device.

```python
import math
import jax
import jax.numpy as jnp
import numpy as np
from jax import lax

C = 128
GROUPS = 32
SLOTS = 32
FR_DEV = 4
TILE_H = 8
TILE_W = 8
CAP = 2
TILES = 1024
FRAMES = 16
HELD = 2048
N_CLIP = 32
N_TM = 4


def draw_tile_frames(key, part):
    key = jax.random.fold_in(key, 11)
    counts = jax.random.randint(key, (TILES,), 1, N_TM + 1)
    first = jnp.arange(TILES, dtype=jnp.int32) % SLOTS == 0
    return (jnp.where(first, N_TM, counts) * FR_DEV).astype(jnp.int32)


def shard_levels(own_key, shape, shards, smallest, high):
    factor_of = 1.0
    for dim, blocks in shards:
        heights = jax.random.uniform(jax.random.fold_in(jax.random.fold_in(own_key, 6), dim), (blocks,), jnp.float32, smallest / len(shards), high / len(shards))
        factor_of = factor_of * jnp.repeat(jnp.exp(heights), shape[dim] // blocks).reshape((-1,) + (1,) * (len(shape) - 1 - dim))
    return factor_of


def routed_block(rng, own, number, rows, number_of, top, most, skew):
    sequence = jax.random.permutation(rng, number_of)
    crowded, usual = shares(number_of, rows * top, most, skew, True), shares(number_of, rows * top, most, skew, False)
    places = jnp.arange(number_of)

    def named(lengths, turn):
        used = int((lengths > 0).sum())
        fixed = max(1, used // 4)
        shifted = fixed + (places - fixed + turn * (used - fixed)) % max(1, number_of - fixed)
        return jnp.zeros((number_of,), jnp.int32).at[sequence[jnp.where(places < fixed, places, shifted)]].set(jnp.asarray(lengths, jnp.int32))

    lengths = jnp.where(number % 4 == 0, named(crowded, number // 4), named(usual, number - number // 4 - 1))
    mixed = jax.random.permutation(jax.random.fold_in(own, 3), number_of)
    giver, receiver = mixed[0:number_of // 2 * 2:2], mixed[1:number_of // 2 * 2:2]
    room = jnp.minimum(lengths[giver] - 1, most - lengths[receiver]) // 2
    room = jnp.where((giver == sequence[0]) | (receiver == sequence[0]) | (lengths[receiver] == 0), 0, jnp.maximum(room, 0))
    shifted = jax.random.randint(jax.random.fold_in(own, 4), (number_of // 2,), 0, 1 << 20) % (room + 1)
    lengths = lengths.at[giver].add(-shifted).at[receiver].add(shifted)
    members = jnp.searchsorted(jnp.cumsum(lengths), jnp.arange(rows * top), side="right").astype(jnp.int32)
    table = members.reshape(top, rows).T
    table = table[jax.random.permutation(jax.random.fold_in(own, 1), rows)]
    turn = jax.random.randint(jax.random.fold_in(own, 2), (rows, 1), 0, top)
    return jnp.take_along_axis(table, (jnp.arange(top)[None, :] + turn) % top, axis=1)


def shares(number_of, total, bound, slope, full):
    weights = [(1 << 20) // math.isqrt(rank ** slope) + 1 for rank in range(1, number_of + 1)]
    largest = bound if full else min(bound, max(-(-total // number_of), total * weights[0] // sum(weights)))
    least = 1 if total - largest >= number_of - 1 else 0
    given, surplus = [largest] + [least] * (number_of - 1), total - largest - least * (number_of - 1)
    while surplus > 0:
        movable = [i for i in range(1, number_of) if given[i] < largest] or [i for i in range(1, number_of) if given[i] < bound]
        pool, remaining = sum([weights[i] for i in movable]), surplus
        for i in movable:
            more = min(bound - given[i], max(1, remaining * weights[i] // pool), surplus)
            given[i] = given[i] + more
            surplus = surplus - more
    return np.array(given)


def gaussian(stream_key, extent, scale, reach, cuts=(), kind=jnp.bfloat16):
    entries = scale * jax.random.normal(stream_key, extent, jnp.float32)
    if cuts:
        entries = entries * shard_levels(stream_key, extent, cuts, -0.22, 0.18)
    return jnp.clip(entries, -reach, reach).astype(kind)


def setup_inputs(seed: int = 0) -> dict:
    key_list = jax.random.split(jax.random.key(seed), 8)
    tiles = gaussian(key_list[0], (TILES, FRAMES, TILE_H, TILE_W, C), 1.0, 6.0, ((0, 32), (1, 4)))
    buckets_keys = jax.random.split(jax.random.fold_in(key_list[1], 1), TILES // SLOTS)
    buckets_turns = jax.random.permutation(jax.random.fold_in(key_list[1], 3), TILES // SLOTS)
    buckets = jax.vmap(lambda own, number: routed_block(jax.random.fold_in(key_list[1], 2), own, number, SLOTS, N_CLIP, 1, CAP, 2))(buckets_keys, buckets_turns).reshape((TILES, 1))
    tile_frames = draw_tile_frames(jax.random.fold_in(key_list[7], 71), 0)
    norm_gain = jnp.clip(jax.random.uniform(key_list[3], (C,), jnp.float32, 0.5, 1.5), 0.5, 1.5)
    norm_shift = gaussian(key_list[4], (C,), 0.5, 3.0, (), jnp.float32)
    conv_weight = gaussian(key_list[5], (3, 3, 3, C, C), (27 * C) ** -0.5, 0.109375)
    conv_bias = gaussian(key_list[6], (C,), 0.3, 2.0, (), jnp.float32)
    return {"tiles": tiles, "buckets": buckets, "tile_frames": tile_frames, "norm_gain": norm_gain, "norm_shift": norm_shift, "conv_weight": conv_weight, "conv_bias": conv_bias}


def encode_tile(pair, norm_gain, norm_shift, conv_weight, conv_bias):
    x, length = pair
    frames, height, width, chans = x.shape
    per = chans // GROUPS
    valid = (jnp.arange(frames, dtype=jnp.int32) < length).astype(jnp.float32)
    mask = valid[:, None, None, None, None]
    xf = x.astype(jnp.float32).reshape(frames, height, width, GROUPS, per)
    count = (length * height * width * per).astype(jnp.float32)
    mean = lax.optimization_barrier(jnp.sum(xf * mask, axis=(0, 1, 2, 4))) / count
    centred = (xf - mean[:, None]) * mask
    var = lax.optimization_barrier(jnp.sum(centred * centred, axis=(0, 1, 2, 4))) / count
    normed = (xf - mean[:, None]) * lax.rsqrt(var + 1e-06)[:, None]
    normed = normed.reshape(frames, height, width, chans) * norm_gain + norm_shift
    act = jax.nn.silu(normed).astype(jnp.bfloat16)
    series = jnp.concatenate([act[:1], act[:1], act], axis=0)
    padded = jnp.pad(series, ((0, 0), (1, 1), (1, 1), (0, 0)))
    total = jnp.zeros((frames * height * width, chans), jnp.float32)
    for step in range(3):
        parts = [padded[step:step + frames, kh:kh + height, kw:kw + width] for kh in range(3) for kw in range(3)]
        cols = jnp.concatenate(parts, axis=-1).reshape(-1, 9 * chans)
        total = total + jnp.dot(cols, conv_weight[step].reshape(9 * chans, chans), preferred_element_type=jnp.float32)
    out = x.astype(jnp.float32) + total.reshape(frames, height, width, chans) + conv_bias
    return (out * valid[:, None, None, None]).astype(jnp.bfloat16)

def reference(tiles, buckets, tile_frames, norm_gain, norm_shift, conv_weight, conv_bias):
    blocks = buckets[:, 0].reshape(N_CLIP, SLOTS)
    onehot = (blocks[:, :, None] == jnp.arange(N_CLIP, dtype=jnp.int32)[None, None, :]).astype(jnp.int32)
    before = jnp.cumsum(onehot, axis=1) - onehot
    rank = lax.optimization_barrier(jnp.sum(before * onehot, axis=2))
    source = jnp.arange(N_CLIP, dtype=jnp.int32)[:, None]
    slot = (blocks * (N_CLIP * CAP) + source * CAP + rank).reshape(-1).astype(jnp.int32)
    encoded = lax.map(lambda pair: encode_tile(pair, norm_gain, norm_shift, conv_weight, conv_bias), (tiles, tile_frames))
    latents = jnp.zeros((HELD,) + tiles.shape[1:], jnp.bfloat16)
    return latents.at[slot].set(encoded)
```

```python
import jax
import jax.numpy as jnp
from jax import lax
from jax.experimental import pallas as pl
from jax.experimental.pallas import tpu as pltpu
from jax.sharding import PartitionSpec as P

MESH = pl.DeviceIdType.MESH
CLIP, TM = 32, 4
TILES, CELLS, CHANS = 32, 64, 128
ROWS = 4 * CELLS
PAIRS = TILES // 2


def target(k):
    me = lax.axis_index("clip")
    core, z, x = me % 2, (me // 2) % 4, me // 8
    dc, a = k // 16, k % 16
    dx = a % 4
    dz = (a + a // 4) % 4
    return (((x + dx) % 4) * 4 + (z + dz) % 4) * 2 + (core + dc) % 2


def place_of(group):
    me = lax.axis_index("clip")
    core, z, x = me % 2, (me // 2) % 4, me // 8
    dc = (group % 2 - core + 2) % 2
    dx = (group // 8 - x + 4) % 4
    dz = ((group // 2) % 4 - z + 4) % 4
    k = dc * 16 + dx + 4 * ((dz - dx + 4) % 4)
    return (k + 31) % 32


def group_sum(v):
    lane = lax.broadcasted_iota(jnp.int32, v.shape, 1)
    for step in (1, 2):
        up = pltpu.roll(v, CHANS - step, 1)
        down = pltpu.roll(v, step, 1)
        v = v + jnp.where((lane // step) % 2 == 0, up, down)
    return v


def column_of(row):
    wide = jnp.broadcast_to(row, (TILES, TILES))
    r = lax.broadcasted_iota(jnp.int32, (TILES, TILES), 0)
    c = lax.broadcasted_iota(jnp.int32, (TILES, TILES), 1)
    return jnp.sum(jnp.where(r == c, wide, 0), axis=1, keepdims=True)


def kernel(
    x_hbm, bucket_ref, frames_ref, frames_smem, gain_ref, shift_ref, w_ref, bias_ref, out_ref,
    x_s, halo_out, halo_in, stats, mean_s, scale_s, acts, wide_w, done, send, table_v, table,
    local_sem, halo_ssem, halo_rsem, stat_ssem, stat_rsem, out_ssem, out_rsem,
):
    me, pos = lax.axis_index("clip"), lax.axis_index("tm")
    x_copy = pltpu.make_async_copy(x_hbm, x_s, local_sem.at[0])
    x_copy.start()

    barrier = pltpu.get_barrier_semaphore()

    @pl.loop(1, CLIP)
    def _(k):
        pl.semaphore_signal(barrier, inc=1, device_id={"clip": target(k)}, device_id_type=MESH)

    for d in range(1, TM):
        pl.semaphore_signal(barrier, inc=1, device_id={"tm": (pos + d) % TM}, device_id_type=MESH)

    step_row = place_of(bucket_ref[...])
    step_col = column_of(step_row)
    r = lax.broadcasted_iota(jnp.int32, (TILES, TILES), 0)
    c = lax.broadcasted_iota(jnp.int32, (TILES, TILES), 1)
    other = jnp.broadcast_to(step_row, (TILES, TILES))
    mine = jnp.broadcast_to(step_col, (TILES, TILES))
    ahead = jnp.where((other < mine) | ((other == mine) & (c < r)), 1, 0)
    place_col = jnp.sum(ahead, axis=1, keepdims=True)
    lanes = lax.broadcasted_iota(jnp.int32, (TILES, CHANS), 1)
    tiles_down = lax.broadcasted_iota(jnp.int32, (TILES, CHANS), 0)
    order = jnp.sum(jnp.where(place_col == lanes, tiles_down, 0), axis=0, keepdims=True)
    start = jnp.sum(jnp.where(step_col < lanes, 1, 0), axis=0, keepdims=True)
    table_v[...] = jnp.zeros_like(table_v)
    table_v[0:1, :] = order
    table_v[1:2, :] = start
    table_copy = pltpu.make_async_copy(table_v, table, local_sem.at[1])
    table_copy.start()

    zeros_w = jnp.zeros((CHANS, CHANS), jnp.bfloat16)
    for kt in range(3):
        for kw in range(3):
            base = (kt * 3 + kw) * 4 * CHANS
            for j in range(4):
                rows = pl.ds(base + j * CHANS, CHANS)
                wide_w[rows, 0:CHANS] = w_ref[kt, j, kw] if j < 3 else zeros_w
                wide_w[rows, CHANS : 2 * CHANS] = w_ref[kt, j - 1, kw] if j > 0 else zeros_w
    pad = jnp.zeros((6, 16, CHANS), jnp.bfloat16)
    for kw in range(3):
        acts[kw, 0, :, 0] = pad
        acts[kw, 1, :, 4] = pad

    x_copy.wait()

    @pl.loop(0, TILES)
    def _(t):
        xf = x_s[t].astype(jnp.float32)
        m = jnp.sum(xf, axis=0, keepdims=True) * (1.0 / ROWS)
        dev = xf - m
        stats[pos, 0, pl.ds(t, 1), :] = m
        stats[pos, 1, pl.ds(t, 1), :] = jnp.sum(dev * dev, axis=0, keepdims=True)

    pl.semaphore_wait(barrier, CLIP - 1 + TM - 1)

    def stat_copy(d, there):
        return pltpu.make_async_remote_copy(
            src_ref=stats.at[pos],
            dst_ref=stats.at[there],
            send_sem=stat_ssem.at[d],
            recv_sem=stat_rsem.at[d],
            device_id={"tm": (pos + d) % TM},
            device_id_type=MESH,
        )

    for d in range(1, TM):
        stat_copy(d, pos).start()

    def halo_copy(m):
        return pltpu.make_async_remote_copy(
            src_ref=halo_out.at[m],
            dst_ref=halo_in.at[m],
            send_sem=halo_ssem.at[m],
            recv_sem=halo_rsem.at[m],
            device_id={"tm": (pos + 1) % TM},
            device_id_type=MESH,
        )

    table_copy.wait()

    @pl.loop(0, PAIRS)
    def _(m):
        for i in range(2):
            halo_out[m, i] = x_s[table[0, 2 * m + i], ROWS // 2 : ROWS, :]
        halo_copy(m).start()

    for d in range(1, TM):
        stat_copy(d, (pos + TM - d) % TM).wait_recv()

    length = column_of(frames_ref[...])
    total = jnp.zeros((TILES, CHANS), jnp.float32)
    weights = [jnp.where(length > 4 * j, 1.0, 0.0) for j in range(TM)]
    parts = weights[0] + weights[1] + weights[2] + weights[3]
    for j in range(TM):
        total = total + stats[j, 0] * weights[j]
    mean = group_sum(total) / (parts * 4.0)
    spread = jnp.zeros((TILES, CHANS), jnp.float32)
    for j in range(TM):
        dev = stats[j, 0] - mean
        spread = spread + (stats[j, 1] + float(ROWS) * (dev * dev)) * weights[j]
    var = group_sum(spread) / (parts * (4.0 * ROWS))
    mean_s[...] = mean
    scale_s[...] = lax.rsqrt(var + 1e-06) * (0.5 * gain_ref[...])

    half_shift = 0.5 * shift_ref[...]
    bias = bias_ref[...]

    def fill(i, slot, at, held):
        got = done[jnp.minimum(at, TILES - 1)]
        send[i, slot] = jnp.where(held, got, jnp.zeros_like(got))

    def out_copy(i):
        return pltpu.make_async_remote_copy(
            src_ref=send.at[i],
            dst_ref=out_ref.at[me],
            send_sem=out_ssem.at[i],
            recv_sem=out_rsem.at[i],
            device_id={"clip": target(i + 1)},
            device_id_type=MESH,
        )

    def fill_both(i):
        first, after = table[1, i], table[1, i + 1]
        fill(i, 0, first, after > first)
        fill(i, 1, first + 1, after > first + 1)

    @pl.loop(0, PAIRS)
    def _(m):
        halo_copy(m).wait_recv()
        tiles = [table[0, 2 * m + i] for i in range(2)]
        series = []
        for i, t in enumerate(tiles):
            xb = x_s[t].astype(jnp.float32).reshape(4, 8, 8, CHANS)
            hb = halo_in[m, i].astype(jnp.float32).reshape(2, 8, 8, CHANS)
            hb = jnp.where(pos == 0, jnp.broadcast_to(xb[0:1], hb.shape), hb)
            raw = jnp.concatenate([hb, xb], axis=0)
            mean_t = mean_s[pl.ds(t, 1), :].reshape(1, 1, 1, CHANS)
            scale_t = scale_s[pl.ds(t, 1), :].reshape(1, 1, 1, CHANS)
            h = (raw - mean_t) * scale_t + half_shift.reshape(1, 1, 1, CHANS)
            series.append((h * jnp.tanh(h) + h).reshape(48, 8, CHANS))
        w = lax.broadcasted_iota(jnp.int32, (48, 8, CHANS), 1)
        for kw in range(3):
            moved = []
            for act in series:
                if kw == 0:
                    act = jnp.where(w == 0, 0.0, pltpu.roll(act, 1, 1))
                if kw == 2:
                    act = jnp.where(w == 7, 0.0, pltpu.roll(act, 7, 1))
                moved.append(act.reshape(6, 8, 1, 8, CHANS))
            both = jnp.concatenate(moved, axis=2).reshape(6, 4, 2, 16, CHANS).astype(jnp.bfloat16)
            acts[kw, 1, :, 0:4] = both[:, :, 0]
            acts[kw, 0, :, 1:5] = both[:, :, 1]
        cols = []
        for kt in range(3):
            for kw in range(3):
                for j in range(4):
                    part = acts[kw, j % 2, kt : kt + 4, j // 2 : j // 2 + 4]
                    cols.append(part.reshape(256, CHANS))
        conv = jnp.dot(
            jnp.concatenate(cols, axis=1), wide_w[...], preferred_element_type=jnp.float32
        )
        rows = [conv[:, 0:CHANS].reshape(4, 4, 2, 8, CHANS), conv[:, CHANS:].reshape(4, 4, 2, 8, CHANS)]
        for i, t in enumerate(tiles):
            xb = x_s[t].astype(jnp.float32)
            both = jnp.concatenate([v[:, :, i : i + 1] for v in rows], axis=2).reshape(ROWS, CHANS)
            res = xb + both + bias
            valid = frames_smem[t] > 4 * pos
            done[2 * m + i] = jnp.where(valid, res, jnp.zeros_like(res)).astype(jnp.bfloat16)
        fill_both(m)
        out_copy(m).start()

    @pl.loop(PAIRS, CLIP - 1)
    def _(i):
        fill_both(i)
        out_copy(i).start()

    fill_both(CLIP - 1)
    own = pltpu.make_async_copy(send.at[CLIP - 1], out_ref.at[me], local_sem.at[2])
    own.start()

    for d in range(1, TM):
        stat_copy(d, pos).wait_send()

    @pl.loop(0, PAIRS)
    def _(m):
        halo_copy(m).wait_send()

    @pl.loop(0, CLIP - 1)
    def _(i):
        out_copy(i).wait_send()

    @pl.loop(0, CLIP - 1)
    def _(i):
        out_copy(i).wait_recv()

    own.wait()


def on_device(tiles, buckets, tile_frames, norm_gain, norm_shift, conv_weight, conv_bias):
    vmem = pl.BlockSpec(memory_space=pltpu.VMEM)
    smem = pl.BlockSpec(memory_space=pltpu.SMEM)
    any_ = pl.BlockSpec(memory_space=pl.ANY)
    bf16, f32 = jnp.bfloat16, jnp.float32
    out = pl.pallas_call(
        kernel,
        out_shape=jax.ShapeDtypeStruct((CLIP, 2, ROWS, CHANS), bf16),
        in_specs=[any_, vmem, vmem, smem, vmem, vmem, vmem, vmem],
        out_specs=any_,
        scratch_shapes=[
            pltpu.VMEM((TILES, ROWS, CHANS), bf16),
            pltpu.VMEM((PAIRS, 2, ROWS // 2, CHANS), bf16),
            pltpu.VMEM((PAIRS, 2, ROWS // 2, CHANS), bf16),
            pltpu.VMEM((TM, 2, TILES, CHANS), f32),
            pltpu.VMEM((TILES, CHANS), f32),
            pltpu.VMEM((TILES, CHANS), f32),
            pltpu.VMEM((3, 2, 6, 5, 16, CHANS), bf16),
            pltpu.VMEM((36 * CHANS, 2 * CHANS), bf16),
            pltpu.VMEM((TILES, ROWS, CHANS), bf16),
            pltpu.VMEM((CLIP, 2, ROWS, CHANS), bf16),
            pltpu.VMEM((8, CHANS), jnp.int32),
            pltpu.SMEM((8, CHANS), jnp.int32),
            pltpu.SemaphoreType.DMA((3,)),
            pltpu.SemaphoreType.DMA((PAIRS,)),
            pltpu.SemaphoreType.DMA((PAIRS,)),
            pltpu.SemaphoreType.DMA((TM,)),
            pltpu.SemaphoreType.DMA((TM,)),
            pltpu.SemaphoreType.DMA((CLIP,)),
            pltpu.SemaphoreType.DMA((CLIP,)),
        ],
        compiler_params=pltpu.CompilerParams(
            collective_id=0, has_side_effects=True, vmem_limit_bytes=40 << 20
        ),
        name="encode_and_send",
    )(
        tiles.reshape(TILES, ROWS, CHANS),
        buckets.reshape(1, TILES),
        tile_frames.reshape(1, TILES),
        tile_frames,
        norm_gain.reshape(1, CHANS),
        norm_shift.reshape(1, CHANS),
        conv_weight,
        conv_bias.reshape(1, CHANS),
    )
    return out.reshape((2 * CLIP,) + tiles.shape[1:])


def solution(mesh):
    in_specs = (P("clip", "tm", None, None, None), P("clip", None), P("clip"), P(), P(), P(), P())
    out_specs = P("clip", "tm", None, None, None)
    return jax.shard_map(
        on_device, mesh=mesh, in_specs=in_specs, out_specs=out_specs, check_vma=False
    )
```

```python
import jax
import jax.numpy as jnp
from jax import lax
from jax.experimental import pallas as pl
from jax.experimental.pallas import tpu as pltpu
from jax.sharding import PartitionSpec as P

MESH = pl.DeviceIdType.MESH
CLIP, TM = 32, 4
TILES, CELLS, CHANS = 32, 64, 128
ROWS = 4 * CELLS
PAIRS = TILES // 2
CHUNKS = 4


def here():
    me = lax.axis_index("clip")
    return lax.div(me, 8), lax.rem(lax.div(me, 2), 4), lax.rem(me, 2)


def target(k):
    x, z, core = here()
    dc, a = lax.div(k, 16), lax.rem(k, 16)
    dx = lax.rem(a, 4)
    dz = a + lax.div(a, 4)
    return (lax.rem(x + dx, 4) * 4 + lax.rem(z + dz, 4)) * 2 + lax.rem(core + dc, 2)


def place_of(group):
    x, z, core = here()
    dc = (group % 2 - core + 2) % 2
    dx = (group // 8 - x + 4) % 4
    dz = ((group // 2) % 4 - z + 4) % 4
    k = dc * 16 + dx + 4 * ((dz - dx + 4) % 4)
    return (k + 31) % 32


def group_sum(v):
    lane = lax.broadcasted_iota(jnp.int32, v.shape, 1)
    for step in (1, 2):
        up = pltpu.roll(v, CHANS - step, 1)
        down = pltpu.roll(v, step, 1)
        v = v + jnp.where((lane // step) % 2 == 0, up, down)
    return v


def column_of(row):
    wide = jnp.broadcast_to(row, (TILES, TILES))
    r = lax.broadcasted_iota(jnp.int32, (TILES, TILES), 0)
    c = lax.broadcasted_iota(jnp.int32, (TILES, TILES), 1)
    return jnp.sum(jnp.where(r == c, wide, 0), axis=1, keepdims=True)


def kernel(
    x_hbm, bucket_hbm, frames_row_hbm, frames_hbm, gain_hbm, shift_hbm, w_hbm, bias_hbm, out_ref,
    x_s, bucket_s, frames_row, frames_smem, gain_ref, shift_ref, bias_ref,
    halo_out, halo_in, stats, mean_s, scale_s, acts, wide_w, done, send, table_v, table,
    x_sem, small_sem, w_sem, local_sem, halo_ssem, halo_rsem, stat_ssem, stat_rsem, out_ssem, out_rsem,
):
    me, pos = lax.axis_index("clip"), lax.axis_index("tm")

    smalls = [
        (bucket_hbm, bucket_s), (frames_row_hbm, frames_row), (frames_hbm, frames_smem),
        (gain_hbm, gain_ref), (shift_hbm, shift_ref), (bias_hbm, bias_ref),
    ]
    small_copies = [
        pltpu.make_async_copy(src, dst, small_sem.at[i]) for i, (src, dst) in enumerate(smalls)
    ]
    small_copies[0].start()
    x_copies = []
    for q in range(CHUNKS):
        part = pl.ds(q * (TILES // CHUNKS), TILES // CHUNKS)
        x_copies.append(pltpu.make_async_copy(x_hbm.at[part], x_s.at[part], x_sem.at[q]))
        x_copies[q].start()

    barrier = pltpu.get_barrier_semaphore()
    for k in range(1, CLIP):
        pl.semaphore_signal(
            barrier, inc=1, device_id={"clip": target(jnp.int32(k))}, device_id_type=MESH
        )
    for d in range(1, TM):
        there = lax.rem(pos + d, TM)
        pl.semaphore_signal(barrier, inc=1, device_id={"tm": there}, device_id_type=MESH)

    for copy in small_copies[1:]:
        copy.start()
    w_copies = []
    for kt in range(3):
        for kw in range(3):
            for odd in range(2):
                copy = pltpu.make_async_copy(
                    w_hbm.at[kt, :, kw],
                    wide_w.at[kt * 3 + kw, pl.ds(odd, 3), :, pl.ds(odd * CHANS, CHANS)],
                    w_sem.at[(kt * 3 + kw) * 2 + odd],
                )
                copy.start()
                w_copies.append(copy)

    small_copies[0].wait()
    step_row = place_of(bucket_s[...])
    step_col = column_of(step_row)
    r = lax.broadcasted_iota(jnp.int32, (TILES, TILES), 0)
    c = lax.broadcasted_iota(jnp.int32, (TILES, TILES), 1)
    other = jnp.broadcast_to(step_row, (TILES, TILES))
    mine = jnp.broadcast_to(step_col, (TILES, TILES))
    ahead = jnp.where((other < mine) | ((other == mine) & (c < r)), 1, 0)
    place_col = jnp.sum(ahead, axis=1, keepdims=True)
    lanes = lax.broadcasted_iota(jnp.int32, (TILES, CHANS), 1)
    tiles_down = lax.broadcasted_iota(jnp.int32, (TILES, CHANS), 0)
    order = jnp.sum(jnp.where(place_col == lanes, tiles_down, 0), axis=0, keepdims=True)
    start = jnp.sum(jnp.where(step_col < lanes, 1, 0), axis=0, keepdims=True)
    table_v[...] = jnp.zeros_like(table_v)
    table_v[0:1, :] = order
    table_v[1:2, :] = start
    table_copy = pltpu.make_async_copy(table_v, table, local_sem.at[1])
    table_copy.start()

    zeros_w = jnp.zeros((9, CHANS, CHANS), jnp.bfloat16)
    wide_w[:, 3, :, 0:CHANS] = zeros_w
    wide_w[:, 0, :, CHANS : 2 * CHANS] = zeros_w
    pad = jnp.zeros((6, 16, CHANS), jnp.bfloat16)
    for kw in range(3):
        acts[kw, 0, :, 0] = pad
        acts[kw, 1, :, 4] = pad

    for q in range(CHUNKS):
        x_copies[q].wait()

        @pl.loop(q * (TILES // CHUNKS), (q + 1) * (TILES // CHUNKS), unroll=4)
        def _(t):
            xf = x_s[t].astype(jnp.float32)
            pivot = xf[0:1]
            dev = (xf - pivot).reshape(ROWS // 8, 8, CHANS)
            first = jnp.sum(jnp.sum(dev, axis=0), axis=0, keepdims=True) * (1.0 / ROWS)
            second = jnp.sum(jnp.sum(dev * dev, axis=0), axis=0, keepdims=True)
            stats[pos, 0, pl.ds(t, 1), :] = pivot + first
            stats[pos, 1, pl.ds(t, 1), :] = jnp.maximum(second - float(ROWS) * (first * first), 0.0)

    pl.semaphore_wait(barrier, CLIP - 1 + TM - 1)

    def stat_copy(d, there):
        return pltpu.make_async_remote_copy(
            src_ref=stats.at[pos],
            dst_ref=stats.at[there],
            send_sem=stat_ssem.at[d],
            recv_sem=stat_rsem.at[d],
            device_id={"tm": lax.rem(pos + d, TM)},
            device_id_type=MESH,
        )

    for d in range(1, TM):
        stat_copy(d, pos).start()

    def halo_copy(m):
        return pltpu.make_async_remote_copy(
            src_ref=halo_out.at[m],
            dst_ref=halo_in.at[m],
            send_sem=halo_ssem.at[m],
            recv_sem=halo_rsem.at[m],
            device_id={"tm": lax.rem(pos + 1, TM)},
            device_id_type=MESH,
        )

    table_copy.wait()

    @pl.loop(0, PAIRS)
    def _(m):
        for i in range(2):
            halo_out[m, i] = x_s[table[0, 2 * m + i], ROWS // 2 : ROWS, :]
        halo_copy(m).start()

    for copy in small_copies[1:]:
        copy.wait()
    for d in range(1, TM):
        stat_copy(d, lax.rem(pos + TM - d, TM)).wait_recv()

    length = column_of(frames_row[...])
    total = jnp.zeros((TILES, CHANS), jnp.float32)
    weights = [jnp.where(length > 4 * j, 1.0, 0.0) for j in range(TM)]
    parts = weights[0] + weights[1] + weights[2] + weights[3]
    for j in range(TM):
        total = total + stats[j, 0] * weights[j]
    mean = group_sum(total) / (parts * 4.0)
    spread = jnp.zeros((TILES, CHANS), jnp.float32)
    for j in range(TM):
        dev = stats[j, 0] - mean
        spread = spread + (stats[j, 1] + float(ROWS) * (dev * dev)) * weights[j]
    var = group_sum(spread) / (parts * (4.0 * ROWS))
    mean_s[...] = mean
    scale_s[...] = lax.rsqrt(var + 1e-06) * (0.5 * gain_ref[...])

    half_shift = 0.5 * shift_ref[...]
    bias = bias_ref[...]
    for copy in w_copies:
        copy.wait()

    def fill(i, slot, at, held):
        got = done[jnp.minimum(at, TILES - 1)]
        send[i, slot] = jnp.where(held, got, jnp.zeros_like(got))

    def out_copy(i):
        return pltpu.make_async_remote_copy(
            src_ref=send.at[i],
            dst_ref=out_ref.at[me],
            send_sem=out_ssem.at[i],
            recv_sem=out_rsem.at[i],
            device_id={"clip": target(i + 1)},
            device_id_type=MESH,
        )

    def fill_both(i):
        first, after = table[1, i], table[1, i + 1]
        fill(i, 0, first, after > first)
        fill(i, 1, first + 1, after > first + 1)

    @pl.loop(0, PAIRS)
    def _(m):
        halo_copy(m).wait_recv()
        tiles = [table[0, 2 * m + i] for i in range(2)]
        series = []
        for i, t in enumerate(tiles):
            xb = x_s[t].astype(jnp.float32).reshape(4, 8, 8, CHANS)
            hb = halo_in[m, i].astype(jnp.float32).reshape(2, 8, 8, CHANS)
            hb = jnp.where(pos == 0, jnp.broadcast_to(xb[0:1], hb.shape), hb)
            raw = jnp.concatenate([hb, xb], axis=0)
            mean_t = mean_s[pl.ds(t, 1), :].reshape(1, 1, 1, CHANS)
            scale_t = scale_s[pl.ds(t, 1), :].reshape(1, 1, 1, CHANS)
            h = (raw - mean_t) * scale_t + half_shift.reshape(1, 1, 1, CHANS)
            series.append((h * jnp.tanh(h) + h).reshape(48, 8, CHANS))
        w = lax.broadcasted_iota(jnp.int32, (48, 8, CHANS), 1)
        for kw in range(3):
            moved = []
            for act in series:
                if kw == 0:
                    act = jnp.where(w == 0, 0.0, pltpu.roll(act, 1, 1))
                if kw == 2:
                    act = jnp.where(w == 7, 0.0, pltpu.roll(act, 7, 1))
                moved.append(act.reshape(6, 8, 1, 8, CHANS))
            both = jnp.concatenate(moved, axis=2).reshape(6, 4, 2, 16, CHANS).astype(jnp.bfloat16)
            acts[kw, 1, :, 0:4] = both[:, :, 0]
            acts[kw, 0, :, 1:5] = both[:, :, 1]
        cols = []
        for kt in range(3):
            for kw in range(3):
                for j in range(4):
                    part = acts[kw, j % 2, kt : kt + 4, j // 2 : j // 2 + 4]
                    cols.append(part.reshape(256, CHANS))
        conv = jnp.dot(
            jnp.concatenate(cols, axis=1),
            wide_w[...].reshape(36 * CHANS, 2 * CHANS),
            preferred_element_type=jnp.float32,
        )
        rows = [conv[:, 0:CHANS].reshape(4, 4, 2, 8, CHANS), conv[:, CHANS:].reshape(4, 4, 2, 8, CHANS)]
        for i, t in enumerate(tiles):
            xb = x_s[t].astype(jnp.float32)
            both = jnp.concatenate([v[:, :, i : i + 1] for v in rows], axis=2).reshape(ROWS, CHANS)
            res = xb + both + bias
            valid = frames_smem[t] > 4 * pos
            done[2 * m + i] = jnp.where(valid, res, jnp.zeros_like(res)).astype(jnp.bfloat16)
        fill_both(m)
        out_copy(m).start()

    @pl.loop(PAIRS, CLIP - 1)
    def _(i):
        fill_both(i)
        out_copy(i).start()

    fill_both(CLIP - 1)
    own = pltpu.make_async_copy(send.at[CLIP - 1], out_ref.at[me], local_sem.at[2])
    own.start()

    for d in range(1, TM):
        stat_copy(d, pos).wait_send()

    @pl.loop(0, PAIRS)
    def _(m):
        halo_copy(m).wait_send()

    @pl.loop(0, CLIP - 1)
    def _(i):
        out_copy(i).wait_send()

    @pl.loop(0, CLIP - 1)
    def _(i):
        out_copy(i).wait_recv()

    own.wait()


def on_device(tiles, buckets, tile_frames, norm_gain, norm_shift, conv_weight, conv_bias):
    hbm = pl.BlockSpec(memory_space=pltpu.HBM)
    any_ = pl.BlockSpec(memory_space=pl.ANY)
    bf16, f32 = jnp.bfloat16, jnp.float32
    out = pl.pallas_call(
        kernel,
        out_shape=jax.ShapeDtypeStruct((CLIP, 2, ROWS, CHANS), bf16),
        in_specs=[hbm] * 8,
        out_specs=any_,
        scratch_shapes=[
            pltpu.VMEM((TILES, ROWS, CHANS), bf16),
            pltpu.VMEM((1, TILES), jnp.int32),
            pltpu.VMEM((1, TILES), jnp.int32),
            pltpu.SMEM((TILES,), jnp.int32),
            pltpu.VMEM((1, CHANS), f32),
            pltpu.VMEM((1, CHANS), f32),
            pltpu.VMEM((1, CHANS), f32),
            pltpu.VMEM((PAIRS, 2, ROWS // 2, CHANS), bf16),
            pltpu.VMEM((PAIRS, 2, ROWS // 2, CHANS), bf16),
            pltpu.VMEM((TM, 2, TILES, CHANS), f32),
            pltpu.VMEM((TILES, CHANS), f32),
            pltpu.VMEM((TILES, CHANS), f32),
            pltpu.VMEM((3, 2, 6, 5, 16, CHANS), bf16),
            pltpu.VMEM((9, 4, CHANS, 2 * CHANS), bf16),
            pltpu.VMEM((TILES, ROWS, CHANS), bf16),
            pltpu.VMEM((CLIP, 2, ROWS, CHANS), bf16),
            pltpu.VMEM((8, CHANS), jnp.int32),
            pltpu.SMEM((8, CHANS), jnp.int32),
            pltpu.SemaphoreType.DMA((CHUNKS,)),
            pltpu.SemaphoreType.DMA((6,)),
            pltpu.SemaphoreType.DMA((18,)),
            pltpu.SemaphoreType.DMA((3,)),
            pltpu.SemaphoreType.DMA((PAIRS,)),
            pltpu.SemaphoreType.DMA((PAIRS,)),
            pltpu.SemaphoreType.DMA((TM,)),
            pltpu.SemaphoreType.DMA((TM,)),
            pltpu.SemaphoreType.DMA((CLIP,)),
            pltpu.SemaphoreType.DMA((CLIP,)),
        ],
        compiler_params=pltpu.CompilerParams(
            collective_id=0, has_side_effects=True, vmem_limit_bytes=40 << 20
        ),
        name="encode_and_send",
    )(
        *[
            pltpu.with_memory_space_constraint(v, pltpu.HBM)
            for v in (
                tiles.reshape(TILES, ROWS, CHANS),
                buckets.reshape(1, TILES),
                tile_frames.reshape(1, TILES),
                tile_frames,
                norm_gain.reshape(1, CHANS),
                norm_shift.reshape(1, CHANS),
                conv_weight,
                conv_bias.reshape(1, CHANS),
            )
        ]
    )
    return out.reshape((2 * CLIP,) + tiles.shape[1:])


def solution(mesh):
    in_specs = (P("clip", "tm", None, None, None), P("clip", None), P("clip"), P(), P(), P(), P())
    out_specs = P("clip", "tm", None, None, None)
    return jax.shard_map(
        on_device, mesh=mesh, in_specs=in_specs, out_specs=out_specs, check_vma=False
    )
```

```python
import jax
import jax.numpy as jnp
from jax import lax
from jax.experimental import pallas as pl
from jax.experimental.pallas import tpu as pltpu
from jax.sharding import PartitionSpec as P

MESH = pl.DeviceIdType.MESH
CLIP, TM = 32, 4
TILES, CELLS, CHANS = 32, 64, 128
ROWS = 4 * CELLS
PAIRS = TILES // 2
CHUNKS = 4
EARLY = 4
SENDS = CLIP - 1 - EARLY


def here():
    me = lax.axis_index("clip")
    return lax.div(me, 8), lax.rem(lax.div(me, 2), 4), lax.rem(me, 2)


def target(k):
    x, z, core = here()
    dc, a = lax.div(k, 16), lax.rem(k, 16)
    dx = lax.rem(a, 4)
    dz = a + lax.div(a, 4)
    return (lax.rem(x + dx, 4) * 4 + lax.rem(z + dz, 4)) * 2 + lax.rem(core + dc, 2)


def origin(k):
    x, z, core = here()
    dc, a = lax.div(k, 16), lax.rem(k, 16)
    dx = lax.rem(a, 4)
    dz = lax.rem(a + lax.div(a, 4), 4)
    return (lax.rem(x + 4 - dx, 4) * 4 + lax.rem(z + 4 - dz, 4)) * 2 + lax.rem(core + 2 - dc, 2)


def place_of(group):
    x, z, core = here()
    dc = (group % 2 - core + 2) % 2
    dx = (group // 8 - x + 4) % 4
    dz = ((group // 2) % 4 - z + 4) % 4
    k = dc * 16 + dx + 4 * ((dz - dx + 4) % 4)
    return (k + 31 - EARLY) % 32


def group_sum(v):
    lane = lax.broadcasted_iota(jnp.int32, v.shape, 1)
    for step in (1, 2):
        up = pltpu.roll(v, CHANS - step, 1)
        down = pltpu.roll(v, step, 1)
        v = v + jnp.where((lane // step) % 2 == 0, up, down)
    return v


def column_of(row):
    wide = jnp.broadcast_to(row, (TILES, TILES))
    r = lax.broadcasted_iota(jnp.int32, (TILES, TILES), 0)
    c = lax.broadcasted_iota(jnp.int32, (TILES, TILES), 1)
    return jnp.sum(jnp.where(r == c, wide, 0), axis=1, keepdims=True)


def kernel(
    x_hbm, bucket_hbm, frames_row_hbm, frames_hbm, gain_hbm, shift_hbm, w_hbm, bias_hbm, out_ref,
    x_s, bucket_s, frames_row, frames_smem, gain_ref, shift_ref, bias_ref,
    halo_out, halo_in, stats, mean_s, scale_s, acts, wide_w, done, send, table_v, table,
    raw_out, raw_in, late_halo, late_done, notes_out, notes_in,
    x_sem, small_sem, w_sem, local_sem, halo_ssem, halo_rsem, stat_ssem, stat_rsem, out_ssem, out_rsem,
    raw_ssem, raw_rsem, late_ssem, late_rsem, notes_ssem, notes_rsem, late_sem,
):
    me, pos = lax.axis_index("clip"), lax.axis_index("tm")

    smalls = [
        (bucket_hbm, bucket_s), (frames_row_hbm, frames_row), (frames_hbm, frames_smem),
        (gain_hbm, gain_ref), (shift_hbm, shift_ref), (bias_hbm, bias_ref),
    ]
    small_copies = [
        pltpu.make_async_copy(src, dst, small_sem.at[i]) for i, (src, dst) in enumerate(smalls)
    ]
    small_copies[0].start()
    x_copies = []
    for q in range(CHUNKS):
        part = pl.ds(q * (TILES // CHUNKS), TILES // CHUNKS)
        x_copies.append(pltpu.make_async_copy(x_hbm.at[part], x_s.at[part], x_sem.at[q]))
        x_copies[q].start()

    barrier = pltpu.get_barrier_semaphore()
    for k in range(1, CLIP):
        pl.semaphore_signal(
            barrier, inc=1, device_id={"clip": target(jnp.int32(k))}, device_id_type=MESH
        )
    for d in range(1, TM):
        there = lax.rem(pos + d, TM)
        pl.semaphore_signal(barrier, inc=1, device_id={"tm": there}, device_id_type=MESH)

    for copy in small_copies[1:]:
        copy.start()
    w_copies = []
    for kt in range(3):
        for kw in range(3):
            for odd in range(2):
                copy = pltpu.make_async_copy(
                    w_hbm.at[kt, :, kw],
                    wide_w.at[kt * 3 + kw, pl.ds(odd, 3), :, pl.ds(odd * CHANS, CHANS)],
                    w_sem.at[(kt * 3 + kw) * 2 + odd],
                )
                copy.start()
                w_copies.append(copy)

    small_copies[0].wait()
    step_row = place_of(bucket_s[...])
    step_col = column_of(step_row)
    r = lax.broadcasted_iota(jnp.int32, (TILES, TILES), 0)
    c = lax.broadcasted_iota(jnp.int32, (TILES, TILES), 1)
    other = jnp.broadcast_to(step_row, (TILES, TILES))
    mine = jnp.broadcast_to(step_col, (TILES, TILES))
    ahead = jnp.where((other < mine) | ((other == mine) & (c < r)), 1, 0)
    place_col = jnp.sum(ahead, axis=1, keepdims=True)
    lanes = lax.broadcasted_iota(jnp.int32, (TILES, CHANS), 1)
    tiles_down = lax.broadcasted_iota(jnp.int32, (TILES, CHANS), 0)
    order = jnp.sum(jnp.where(place_col == lanes, tiles_down, 0), axis=0, keepdims=True)
    start = jnp.sum(jnp.where(step_col < lanes, 1, 0), axis=0, keepdims=True)
    table_v[...] = jnp.zeros_like(table_v)
    table_v[0:1, :] = order
    table_v[1:2, :] = start
    table_copy = pltpu.make_async_copy(table_v, table, local_sem.at[1])
    table_copy.start()

    zeros_w = jnp.zeros((9, CHANS, CHANS), jnp.bfloat16)
    wide_w[:, 3, :, 0:CHANS] = zeros_w
    wide_w[:, 0, :, CHANS : 2 * CHANS] = zeros_w
    pad = jnp.zeros((6, 16, CHANS), jnp.bfloat16)
    for kw in range(3):
        acts[kw, 0, :, 0] = pad
        acts[kw, 1, :, 4] = pad

    def raw_copy(j):
        return pltpu.make_async_remote_copy(
            src_ref=raw_out.at[j],
            dst_ref=raw_in.at[j],
            send_sem=raw_ssem.at[j],
            recv_sem=raw_rsem.at[j],
            device_id={"clip": target(j + 1)},
            device_id_type=MESH,
        )

    def early_slots(j):
        first, after = table[1, CLIP - EARLY + j], table[1, CLIP - EARLY + 1 + j]
        places = [first, first + 1]
        return [(table[0, jnp.minimum(at, TILES - 1)], after > at) for at in places]

    table_copy.wait()
    for copy in x_copies:
        copy.wait()

    @pl.loop(0, EARLY)
    def _(j):
        for i, (t, _) in enumerate(early_slots(j)):
            raw_out[j, i] = x_s[t]

    pl.semaphore_wait(barrier, CLIP - 1 + TM - 1)

    @pl.loop(0, EARLY)
    def _(j):
        raw_copy(j).start()

    def stat_copy(d, there):
        return pltpu.make_async_remote_copy(
            src_ref=stats.at[pos],
            dst_ref=stats.at[there],
            send_sem=stat_ssem.at[d],
            recv_sem=stat_rsem.at[d],
            device_id={"tm": lax.rem(pos + d, TM)},
            device_id_type=MESH,
        )

    for q in range(CHUNKS):
        @pl.loop(q * (TILES // CHUNKS), (q + 1) * (TILES // CHUNKS), unroll=4)
        def _(t):
            xf = x_s[t].astype(jnp.float32)
            pivot = xf[0:1]
            dev = (xf - pivot).reshape(ROWS // 8, 8, CHANS)
            first = jnp.sum(jnp.sum(dev, axis=0), axis=0, keepdims=True) * (1.0 / ROWS)
            second = jnp.sum(jnp.sum(dev * dev, axis=0), axis=0, keepdims=True)
            stats[pos, 0, pl.ds(t, 1), :] = pivot + first
            stats[pos, 1, pl.ds(t, 1), :] = jnp.maximum(second - float(ROWS) * (first * first), 0.0)

    for d in range(1, TM):
        stat_copy(d, pos).start()

    def halo_copy(m):
        return pltpu.make_async_remote_copy(
            src_ref=halo_out.at[m],
            dst_ref=halo_in.at[m],
            send_sem=halo_ssem.at[m],
            recv_sem=halo_rsem.at[m],
            device_id={"tm": lax.rem(pos + 1, TM)},
            device_id_type=MESH,
        )

    @pl.loop(0, PAIRS)
    def _(m):
        for i in range(2):
            halo_out[m, i] = x_s[table[0, 2 * m + i], ROWS // 2 : ROWS, :]
        halo_copy(m).start()

    for copy in small_copies[1:]:
        copy.wait()
    for d in range(1, TM):
        stat_copy(d, lax.rem(pos + TM - d, TM)).wait_recv()

    length = column_of(frames_row[...])
    total = jnp.zeros((TILES, CHANS), jnp.float32)
    weights = [jnp.where(length > 4 * j, 1.0, 0.0) for j in range(TM)]
    parts = weights[0] + weights[1] + weights[2] + weights[3]
    for j in range(TM):
        total = total + stats[j, 0] * weights[j]
    mean = group_sum(total) / (parts * 4.0)
    spread = jnp.zeros((TILES, CHANS), jnp.float32)
    for j in range(TM):
        dev = stats[j, 0] - mean
        spread = spread + (stats[j, 1] + float(ROWS) * (dev * dev)) * weights[j]
    var = group_sum(spread) / (parts * (4.0 * ROWS))
    mean_s[...] = mean
    scale_s[...] = lax.rsqrt(var + 1e-06) * (0.5 * gain_ref[...])

    half_shift = 0.5 * shift_ref[...]
    bias = bias_ref[...]
    for copy in w_copies:
        copy.wait()

    def fill(i, slot, at, held):
        got = done[jnp.minimum(at, TILES - 1)]
        send[i, slot] = jnp.where(held, got, jnp.zeros_like(got))

    def out_copy(i):
        return pltpu.make_async_remote_copy(
            src_ref=send.at[i],
            dst_ref=out_ref.at[me],
            send_sem=out_ssem.at[i],
            recv_sem=out_rsem.at[i],
            device_id={"clip": target(i + 1 + EARLY)},
            device_id_type=MESH,
        )

    def fill_both(i):
        first, after = table[1, i], table[1, i + 1]
        fill(i, 0, first, after > first)
        fill(i, 1, first + 1, after > first + 1)

    def unit(tiles):
        series = []
        for cells, before, mean_t, scale_t in tiles:
            xb = cells.astype(jnp.float32).reshape(4, 8, 8, CHANS)
            hb = before.astype(jnp.float32).reshape(2, 8, 8, CHANS)
            hb = jnp.where(pos == 0, jnp.broadcast_to(xb[0:1], hb.shape), hb)
            raw = jnp.concatenate([hb, xb], axis=0)
            mean_t = mean_t.reshape(1, 1, 1, CHANS)
            scale_t = scale_t.reshape(1, 1, 1, CHANS)
            h = (raw - mean_t) * scale_t + half_shift.reshape(1, 1, 1, CHANS)
            series.append((h * jnp.tanh(h) + h).reshape(48, 8, CHANS))
        w = lax.broadcasted_iota(jnp.int32, (48, 8, CHANS), 1)
        for kw in range(3):
            moved = []
            for act in series:
                if kw == 0:
                    act = jnp.where(w == 0, 0.0, pltpu.roll(act, 1, 1))
                if kw == 2:
                    act = jnp.where(w == 7, 0.0, pltpu.roll(act, 7, 1))
                moved.append(act.reshape(6, 8, 1, 8, CHANS))
            both = jnp.concatenate(moved, axis=2).reshape(6, 4, 2, 16, CHANS).astype(jnp.bfloat16)
            acts[kw, 1, :, 0:4] = both[:, :, 0]
            acts[kw, 0, :, 1:5] = both[:, :, 1]
        cols = []
        for kt in range(3):
            for kw in range(3):
                for j in range(4):
                    part = acts[kw, j % 2, kt : kt + 4, j // 2 : j // 2 + 4]
                    cols.append(part.reshape(256, CHANS))
        conv = jnp.dot(
            jnp.concatenate(cols, axis=1),
            wide_w[...].reshape(36 * CHANS, 2 * CHANS),
            preferred_element_type=jnp.float32,
        )
        rows = [
            conv[:, 0:CHANS].reshape(4, 4, 2, 8, CHANS),
            conv[:, CHANS:].reshape(4, 4, 2, 8, CHANS),
        ]
        results = []
        for i, (cells, _, _, _) in enumerate(tiles):
            both = jnp.concatenate([v[:, :, i : i + 1] for v in rows], axis=2)
            results.append(cells.astype(jnp.float32) + both.reshape(ROWS, CHANS) + bias)
        return results

    def late_copy(j):
        return pltpu.make_async_remote_copy(
            src_ref=raw_in.at[j, :, pl.ds(ROWS // 2, ROWS // 2)],
            dst_ref=late_halo.at[j],
            send_sem=late_ssem.at[j],
            recv_sem=late_rsem.at[j],
            device_id={"tm": lax.rem(pos + 1, TM)},
            device_id_type=MESH,
        )

    def notes_copy(j):
        return pltpu.make_async_remote_copy(
            src_ref=notes_out.at[j],
            dst_ref=notes_in.at[j],
            send_sem=notes_ssem.at[j],
            recv_sem=notes_rsem.at[j],
            device_id={"clip": target(j + 1)},
            device_id_type=MESH,
        )

    @pl.loop(0, EARLY)
    def _(j):
        notes_out[j] = jnp.zeros((8, CHANS), jnp.float32)
        for i, (t, held) in enumerate(early_slots(j)):
            notes_out[j, i : i + 1] = mean_s[pl.ds(t, 1), :]
            notes_out[j, 2 + i : 3 + i] = scale_s[pl.ds(t, 1), :]
            valid = held & (frames_smem[t] > 4 * pos)
            notes_out[j, 4 + i : 5 + i] = jnp.where(valid, jnp.ones((1, CHANS)), jnp.zeros((1, CHANS)))
        notes_copy(j).start()

    @pl.loop(0, PAIRS)
    def _(m):
        halo_copy(m).wait_recv()
        tiles = [table[0, 2 * m + i] for i in range(2)]
        results = unit(
            [
                (x_s[t], halo_in[m, i], mean_s[pl.ds(t, 1), :], scale_s[pl.ds(t, 1), :])
                for i, t in enumerate(tiles)
            ]
        )
        for i, t in enumerate(tiles):
            valid = frames_smem[t] > 4 * pos
            res = results[i]
            done[2 * m + i] = jnp.where(valid, res, jnp.zeros_like(res)).astype(jnp.bfloat16)
        fill_both(m)
        out_copy(m).start()

        @pl.when(m >= PAIRS - EARLY)
        def _():
            raw_copy(m - (PAIRS - EARLY)).wait_recv()
            late_copy(m - (PAIRS - EARLY)).start()

    @pl.loop(PAIRS, SENDS)
    def _(i):
        fill_both(i)
        out_copy(i).start()

    fill_both(SENDS)
    own = pltpu.make_async_copy(send.at[SENDS], out_ref.at[me], local_sem.at[2])
    own.start()

    def late_out(j):
        return pltpu.make_async_copy(late_done.at[j], out_ref.at[origin(j + 1)], late_sem.at[j])

    @pl.loop(0, EARLY)
    def _(j):
        late_copy(j).wait_recv()
        notes_copy(j).wait_recv()
        results = unit(
            [
                (raw_in[j, i], late_halo[j, i], notes_in[j, i : i + 1], notes_in[j, 2 + i : 3 + i])
                for i in range(2)
            ]
        )
        for i in range(2):
            valid = notes_in[j, 4 + i : 5 + i] > 0.5
            res = results[i]
            late_done[j, i] = jnp.where(valid, res, jnp.zeros_like(res)).astype(jnp.bfloat16)
        late_out(j).start()

    for d in range(1, TM):
        stat_copy(d, pos).wait_send()

    @pl.loop(0, PAIRS)
    def _(m):
        halo_copy(m).wait_send()

    @pl.loop(0, EARLY)
    def _(j):
        raw_copy(j).wait_send()
        late_copy(j).wait_send()
        notes_copy(j).wait_send()
        late_out(j).wait()

    own.wait()

    @pl.loop(0, SENDS)
    def _(i):
        out_copy(i).wait_send()

    @pl.loop(0, SENDS)
    def _(i):
        out_copy(i).wait_recv()


def on_device(tiles, buckets, tile_frames, norm_gain, norm_shift, conv_weight, conv_bias):
    hbm = pl.BlockSpec(memory_space=pltpu.HBM)
    any_ = pl.BlockSpec(memory_space=pl.ANY)
    bf16, f32 = jnp.bfloat16, jnp.float32
    out = pl.pallas_call(
        kernel,
        out_shape=jax.ShapeDtypeStruct((CLIP, 2, ROWS, CHANS), bf16),
        in_specs=[hbm] * 8,
        out_specs=any_,
        scratch_shapes=[
            pltpu.VMEM((TILES, ROWS, CHANS), bf16),
            pltpu.VMEM((1, TILES), jnp.int32),
            pltpu.VMEM((1, TILES), jnp.int32),
            pltpu.SMEM((TILES,), jnp.int32),
            pltpu.VMEM((1, CHANS), f32),
            pltpu.VMEM((1, CHANS), f32),
            pltpu.VMEM((1, CHANS), f32),
            pltpu.VMEM((PAIRS, 2, ROWS // 2, CHANS), bf16),
            pltpu.VMEM((PAIRS, 2, ROWS // 2, CHANS), bf16),
            pltpu.VMEM((TM, 2, TILES, CHANS), f32),
            pltpu.VMEM((TILES, CHANS), f32),
            pltpu.VMEM((TILES, CHANS), f32),
            pltpu.VMEM((3, 2, 6, 5, 16, CHANS), bf16),
            pltpu.VMEM((9, 4, CHANS, 2 * CHANS), bf16),
            pltpu.VMEM((TILES, ROWS, CHANS), bf16),
            pltpu.VMEM((SENDS + 1, 2, ROWS, CHANS), bf16),
            pltpu.VMEM((8, CHANS), jnp.int32),
            pltpu.SMEM((8, CHANS), jnp.int32),
            pltpu.VMEM((EARLY, 2, ROWS, CHANS), bf16),
            pltpu.VMEM((EARLY, 2, ROWS, CHANS), bf16),
            pltpu.VMEM((EARLY, 2, ROWS // 2, CHANS), bf16),
            pltpu.VMEM((EARLY, 2, ROWS, CHANS), bf16),
            pltpu.VMEM((EARLY, 8, CHANS), f32),
            pltpu.VMEM((EARLY, 8, CHANS), f32),
            pltpu.SemaphoreType.DMA((CHUNKS,)),
            pltpu.SemaphoreType.DMA((6,)),
            pltpu.SemaphoreType.DMA((18,)),
            pltpu.SemaphoreType.DMA((3,)),
            pltpu.SemaphoreType.DMA((PAIRS,)),
            pltpu.SemaphoreType.DMA((PAIRS,)),
            pltpu.SemaphoreType.DMA((TM,)),
            pltpu.SemaphoreType.DMA((TM,)),
            pltpu.SemaphoreType.DMA((SENDS,)),
            pltpu.SemaphoreType.DMA((SENDS,)),
            pltpu.SemaphoreType.DMA((EARLY,)),
            pltpu.SemaphoreType.DMA((EARLY,)),
            pltpu.SemaphoreType.DMA((EARLY,)),
            pltpu.SemaphoreType.DMA((EARLY,)),
            pltpu.SemaphoreType.DMA((EARLY,)),
            pltpu.SemaphoreType.DMA((EARLY,)),
            pltpu.SemaphoreType.DMA((EARLY,)),
        ],
        compiler_params=pltpu.CompilerParams(
            collective_id=0, has_side_effects=True, vmem_limit_bytes=40 << 20
        ),
        name="encode_and_send",
    )(
        *[
            pltpu.with_memory_space_constraint(v, pltpu.HBM)
            for v in (
                tiles.reshape(TILES, ROWS, CHANS),
                buckets.reshape(1, TILES),
                tile_frames.reshape(1, TILES),
                tile_frames,
                norm_gain.reshape(1, CHANS),
                norm_shift.reshape(1, CHANS),
                conv_weight,
                conv_bias.reshape(1, CHANS),
            )
        ]
    )
    return out.reshape((2 * CLIP,) + tiles.shape[1:])


def solution(mesh):
    in_specs = (P("clip", "tm", None, None, None), P("clip", None), P("clip"), P(), P(), P(), P())
    out_specs = P("clip", "tm", None, None, None)
    return jax.shard_map(
        on_device, mesh=mesh, in_specs=in_specs, out_specs=out_specs, check_vma=False
    )
```

```python
import jax
import jax.numpy as jnp
from jax import lax
from jax.experimental import pallas as pl
from jax.experimental.pallas import tpu as pltpu
from jax.sharding import PartitionSpec as P

MESH = pl.DeviceIdType.MESH
CLIP, TM = 32, 4
TILES, CELLS, CHANS = 32, 64, 128
ROWS = 4 * CELLS
PAIRS = TILES // 2
CHUNKS = 4
EARLY = 6
SENDS = CLIP - 1 - EARLY


SETS = [
    [(2, 2)],
    [(1, 1), (3, 3)],
    [(1, 3), (3, 1)],
    [(2, 0), (0, 2)],
    [(1, 2), (3, 0)],
    [(3, 2), (1, 0)],
    [(2, 1), (0, 3)],
    [(2, 3), (0, 1)],
]
ORDER = [(dx, dz, dc) for s in SETS for dc in range(2) for dx, dz in s] + [(0, 0, 1)]
assert sorted(ORDER) == [(x, z, c) for x in range(4) for z in range(4) for c in range(2)][1:]


def packed(values):
    return [sum(v << 2 * i for i, v in enumerate(values[h : h + 15])) for h in (0, 15, 30)]


WORDS = [packed([o[i] for o in ORDER]) for i in range(3)]


def here():
    me = lax.axis_index("clip")
    return lax.div(me, 8), lax.rem(lax.div(me, 2), 4), lax.rem(me, 2)


def offset(k):
    part, by = lax.div(k, 15), 2 * lax.rem(k, 15)
    words = [jnp.where(part == 0, w[0], jnp.where(part == 1, w[1], w[2])) for w in WORDS]
    return [lax.rem(lax.shift_right_logical(w, by), 4) for w in words]


def target(k):
    x, z, core = here()
    dx, dz, dc = offset(jnp.int32(k))
    return (lax.rem(x + dx, 4) * 4 + lax.rem(z + dz, 4)) * 2 + lax.rem(core + dc, 2)


def origin(k):
    x, z, core = here()
    dx, dz, dc = offset(jnp.int32(k))
    return (lax.rem(x + 4 - dx, 4) * 4 + lax.rem(z + 4 - dz, 4)) * 2 + lax.rem(core + 2 - dc, 2)


def place_of(group):
    x, z, core = here()
    step = jnp.full(group.shape, SENDS, jnp.int32)
    for k, (dx, dz, dc) in enumerate(ORDER):
        there = (lax.rem(x + dx, 4) * 4 + lax.rem(z + dz, 4)) * 2 + lax.rem(core + dc, 2)
        step = jnp.where(group == there, k - EARLY if k >= EARLY else SENDS + 1 + k, step)
    return step


def group_sum(v):
    lane = lax.broadcasted_iota(jnp.int32, v.shape, 1)
    for step in (1, 2):
        up = pltpu.roll(v, CHANS - step, 1)
        down = pltpu.roll(v, step, 1)
        v = v + jnp.where((lane // step) % 2 == 0, up, down)
    return v


def column_of(row):
    wide = jnp.broadcast_to(row, (TILES, TILES))
    r = lax.broadcasted_iota(jnp.int32, (TILES, TILES), 0)
    c = lax.broadcasted_iota(jnp.int32, (TILES, TILES), 1)
    return jnp.sum(jnp.where(r == c, wide, 0), axis=1, keepdims=True)


def kernel(
    x_hbm, bucket_hbm, frames_row_hbm, frames_hbm, gain_hbm, shift_hbm, w_hbm, bias_hbm, out_ref,
    x_s, bucket_s, frames_row, frames_smem, gain_ref, shift_ref, bias_ref,
    halo_out, halo_in, stats, mean_s, scale_s, acts, wide_w, done, send, table_v, table,
    raw_out, raw_in, late_halo, late_done, notes_out, notes_in,
    x_sem, small_sem, w_sem, local_sem, halo_ssem, halo_rsem, stat_ssem, stat_rsem, out_ssem, out_rsem,
    raw_ssem, raw_rsem, late_ssem, late_rsem, notes_ssem, notes_rsem, late_sem,
):
    me, pos = lax.axis_index("clip"), lax.axis_index("tm")

    smalls = [
        (bucket_hbm, bucket_s), (frames_row_hbm, frames_row), (frames_hbm, frames_smem),
        (gain_hbm, gain_ref), (shift_hbm, shift_ref), (bias_hbm, bias_ref),
    ]
    small_copies = [
        pltpu.make_async_copy(src, dst, small_sem.at[i]) for i, (src, dst) in enumerate(smalls)
    ]
    small_copies[0].start()
    x_copies = []
    for q in range(CHUNKS):
        part = pl.ds(q * (TILES // CHUNKS), TILES // CHUNKS)
        x_copies.append(pltpu.make_async_copy(x_hbm.at[part], x_s.at[part], x_sem.at[q]))
        x_copies[q].start()

    barrier = pltpu.get_barrier_semaphore()
    x, z, core = here()
    for dx, dz, dc in ORDER:
        there = (lax.rem(x + dx, 4) * 4 + lax.rem(z + dz, 4)) * 2 + lax.rem(core + dc, 2)
        pl.semaphore_signal(barrier, inc=1, device_id={"clip": there}, device_id_type=MESH)
    for d in range(1, TM):
        there = lax.rem(pos + d, TM)
        pl.semaphore_signal(barrier, inc=1, device_id={"tm": there}, device_id_type=MESH)

    for copy in small_copies[1:]:
        copy.start()
    w_copies = []
    for kt in range(3):
        for kw in range(3):
            for odd in range(2):
                copy = pltpu.make_async_copy(
                    w_hbm.at[kt, :, kw],
                    wide_w.at[kt * 3 + kw, pl.ds(odd, 3), :, pl.ds(odd * CHANS, CHANS)],
                    w_sem.at[(kt * 3 + kw) * 2 + odd],
                )
                copy.start()
                w_copies.append(copy)

    small_copies[0].wait()
    step_row = place_of(bucket_s[...])
    step_col = column_of(step_row)
    r = lax.broadcasted_iota(jnp.int32, (TILES, TILES), 0)
    c = lax.broadcasted_iota(jnp.int32, (TILES, TILES), 1)
    other = jnp.broadcast_to(step_row, (TILES, TILES))
    mine = jnp.broadcast_to(step_col, (TILES, TILES))
    ahead = jnp.where((other < mine) | ((other == mine) & (c < r)), 1, 0)
    place_col = jnp.sum(ahead, axis=1, keepdims=True)
    lanes = lax.broadcasted_iota(jnp.int32, (TILES, CHANS), 1)
    tiles_down = lax.broadcasted_iota(jnp.int32, (TILES, CHANS), 0)
    order = jnp.sum(jnp.where(place_col == lanes, tiles_down, 0), axis=0, keepdims=True)
    start = jnp.sum(jnp.where(step_col < lanes, 1, 0), axis=0, keepdims=True)
    table_v[...] = jnp.zeros_like(table_v)
    table_v[0:1, :] = order
    table_v[1:2, :] = start
    table_copy = pltpu.make_async_copy(table_v, table, local_sem.at[1])
    table_copy.start()

    zeros_w = jnp.zeros((9, CHANS, CHANS), jnp.bfloat16)
    wide_w[:, 3, :, 0:CHANS] = zeros_w
    wide_w[:, 0, :, CHANS : 2 * CHANS] = zeros_w
    pad = jnp.zeros((6, 16, CHANS), jnp.bfloat16)
    for kw in range(3):
        acts[kw, 0, :, 0] = pad
        acts[kw, 1, :, 4] = pad

    def raw_copy(j):
        return pltpu.make_async_remote_copy(
            src_ref=raw_out.at[j],
            dst_ref=raw_in.at[j],
            send_sem=raw_ssem.at[j],
            recv_sem=raw_rsem.at[j],
            device_id={"clip": target(j)},
            device_id_type=MESH,
        )

    def early_slots(j):
        first, after = table[1, CLIP - EARLY + j], table[1, CLIP - EARLY + 1 + j]
        places = [first, first + 1]
        return [(table[0, jnp.minimum(at, TILES - 1)], after > at) for at in places]

    table_copy.wait()
    for copy in x_copies:
        copy.wait()

    @pl.loop(0, EARLY)
    def _(j):
        for i, (t, _) in enumerate(early_slots(j)):
            raw_out[j, i] = x_s[t]

    pl.semaphore_wait(barrier, CLIP - 1 + TM - 1)

    @pl.loop(0, EARLY)
    def _(j):
        raw_copy(j).start()

    def stat_copy(d, there):
        return pltpu.make_async_remote_copy(
            src_ref=stats.at[pos],
            dst_ref=stats.at[there],
            send_sem=stat_ssem.at[d],
            recv_sem=stat_rsem.at[d],
            device_id={"tm": lax.rem(pos + d, TM)},
            device_id_type=MESH,
        )

    for q in range(CHUNKS):
        @pl.loop(q * (TILES // CHUNKS), (q + 1) * (TILES // CHUNKS), unroll=4)
        def _(t):
            xf = x_s[t].astype(jnp.float32)
            pivot = xf[0:1]
            dev = (xf - pivot).reshape(ROWS // 8, 8, CHANS)
            first = jnp.sum(jnp.sum(dev, axis=0), axis=0, keepdims=True) * (1.0 / ROWS)
            second = jnp.sum(jnp.sum(dev * dev, axis=0), axis=0, keepdims=True)
            stats[pos, 0, pl.ds(t, 1), :] = pivot + first
            stats[pos, 1, pl.ds(t, 1), :] = jnp.maximum(second - float(ROWS) * (first * first), 0.0)

    for d in range(1, TM):
        stat_copy(d, pos).start()

    def halo_copy(m):
        return pltpu.make_async_remote_copy(
            src_ref=halo_out.at[m],
            dst_ref=halo_in.at[m],
            send_sem=halo_ssem.at[m],
            recv_sem=halo_rsem.at[m],
            device_id={"tm": lax.rem(pos + 1, TM)},
            device_id_type=MESH,
        )

    @pl.loop(0, PAIRS)
    def _(m):
        for i in range(2):
            halo_out[m, i] = x_s[table[0, 2 * m + i], ROWS // 2 : ROWS, :]
        halo_copy(m).start()

    for copy in small_copies[1:]:
        copy.wait()
    for d in range(1, TM):
        stat_copy(d, lax.rem(pos + TM - d, TM)).wait_recv()

    length = column_of(frames_row[...])
    total = jnp.zeros((TILES, CHANS), jnp.float32)
    weights = [jnp.where(length > 4 * j, 1.0, 0.0) for j in range(TM)]
    parts = weights[0] + weights[1] + weights[2] + weights[3]
    for j in range(TM):
        total = total + stats[j, 0] * weights[j]
    mean = group_sum(total) / (parts * 4.0)
    spread = jnp.zeros((TILES, CHANS), jnp.float32)
    for j in range(TM):
        dev = stats[j, 0] - mean
        spread = spread + (stats[j, 1] + float(ROWS) * (dev * dev)) * weights[j]
    var = group_sum(spread) / (parts * (4.0 * ROWS))
    mean_s[...] = mean
    scale_s[...] = lax.rsqrt(var + 1e-06) * (0.5 * gain_ref[...])

    half_shift = 0.5 * shift_ref[...]
    bias = bias_ref[...]
    for copy in w_copies:
        copy.wait()

    def fill(i, slot, at, held):
        got = done[jnp.minimum(at, TILES - 1)]
        send[i, slot] = jnp.where(held, got, jnp.zeros_like(got))

    def out_copy(i):
        return pltpu.make_async_remote_copy(
            src_ref=send.at[i],
            dst_ref=out_ref.at[me],
            send_sem=out_ssem.at[i],
            recv_sem=out_rsem.at[i],
            device_id={"clip": target(i + EARLY)},
            device_id_type=MESH,
        )

    def fill_both(i):
        first, after = table[1, i], table[1, i + 1]
        fill(i, 0, first, after > first)
        fill(i, 1, first + 1, after > first + 1)

    def unit(tiles):
        series = []
        for cells, before, mean_t, scale_t in tiles:
            xb = cells.astype(jnp.float32).reshape(4, 8, 8, CHANS)
            hb = before.astype(jnp.float32).reshape(2, 8, 8, CHANS)
            hb = jnp.where(pos == 0, jnp.broadcast_to(xb[0:1], hb.shape), hb)
            raw = jnp.concatenate([hb, xb], axis=0)
            mean_t = mean_t.reshape(1, 1, 1, CHANS)
            scale_t = scale_t.reshape(1, 1, 1, CHANS)
            h = (raw - mean_t) * scale_t + half_shift.reshape(1, 1, 1, CHANS)
            series.append((h * jnp.tanh(h) + h).reshape(48, 8, CHANS))
        w = lax.broadcasted_iota(jnp.int32, (48, 8, CHANS), 1)
        for kw in range(3):
            moved = []
            for act in series:
                if kw == 0:
                    act = jnp.where(w == 0, 0.0, pltpu.roll(act, 1, 1))
                if kw == 2:
                    act = jnp.where(w == 7, 0.0, pltpu.roll(act, 7, 1))
                moved.append(act.reshape(6, 8, 1, 8, CHANS))
            both = jnp.concatenate(moved, axis=2).reshape(6, 4, 2, 16, CHANS).astype(jnp.bfloat16)
            acts[kw, 1, :, 0:4] = both[:, :, 0]
            acts[kw, 0, :, 1:5] = both[:, :, 1]
        cols = []
        for kt in range(3):
            for kw in range(3):
                for j in range(4):
                    part = acts[kw, j % 2, kt : kt + 4, j // 2 : j // 2 + 4]
                    cols.append(part.reshape(256, CHANS))
        conv = jnp.dot(
            jnp.concatenate(cols, axis=1),
            wide_w[...].reshape(36 * CHANS, 2 * CHANS),
            preferred_element_type=jnp.float32,
        )
        rows = [
            conv[:, 0:CHANS].reshape(4, 4, 2, 8, CHANS),
            conv[:, CHANS:].reshape(4, 4, 2, 8, CHANS),
        ]
        results = []
        for i, (cells, _, _, _) in enumerate(tiles):
            both = jnp.concatenate([v[:, :, i : i + 1] for v in rows], axis=2)
            results.append(cells.astype(jnp.float32) + both.reshape(ROWS, CHANS) + bias)
        return results

    def late_copy(j):
        return pltpu.make_async_remote_copy(
            src_ref=raw_in.at[j, :, pl.ds(ROWS // 2, ROWS // 2)],
            dst_ref=late_halo.at[j],
            send_sem=late_ssem.at[j],
            recv_sem=late_rsem.at[j],
            device_id={"tm": lax.rem(pos + 1, TM)},
            device_id_type=MESH,
        )

    def notes_copy(j):
        return pltpu.make_async_remote_copy(
            src_ref=notes_out.at[j],
            dst_ref=notes_in.at[j],
            send_sem=notes_ssem.at[j],
            recv_sem=notes_rsem.at[j],
            device_id={"clip": target(j)},
            device_id_type=MESH,
        )

    @pl.loop(0, EARLY)
    def _(j):
        notes_out[j] = jnp.zeros((8, CHANS), jnp.float32)
        for i, (t, held) in enumerate(early_slots(j)):
            notes_out[j, i : i + 1] = mean_s[pl.ds(t, 1), :]
            notes_out[j, 2 + i : 3 + i] = scale_s[pl.ds(t, 1), :]
            valid = held & (frames_smem[t] > 4 * pos)
            notes_out[j, 4 + i : 5 + i] = jnp.where(valid, jnp.ones((1, CHANS)), jnp.zeros((1, CHANS)))
        notes_copy(j).start()

    @pl.loop(0, PAIRS)
    def _(m):
        halo_copy(m).wait_recv()
        tiles = [table[0, 2 * m + i] for i in range(2)]
        results = unit(
            [
                (x_s[t], halo_in[m, i], mean_s[pl.ds(t, 1), :], scale_s[pl.ds(t, 1), :])
                for i, t in enumerate(tiles)
            ]
        )
        for i, t in enumerate(tiles):
            valid = frames_smem[t] > 4 * pos
            res = results[i]
            done[2 * m + i] = jnp.where(valid, res, jnp.zeros_like(res)).astype(jnp.bfloat16)
        fill_both(m)
        out_copy(m).start()

        @pl.when(m >= PAIRS - EARLY)
        def _():
            raw_copy(m - (PAIRS - EARLY)).wait_recv()
            late_copy(m - (PAIRS - EARLY)).start()

    @pl.loop(PAIRS, SENDS)
    def _(i):
        fill_both(i)
        out_copy(i).start()

    fill_both(SENDS)
    own = pltpu.make_async_copy(send.at[SENDS], out_ref.at[me], local_sem.at[2])
    own.start()

    def late_out(j):
        return pltpu.make_async_copy(late_done.at[j], out_ref.at[origin(j)], late_sem.at[j])

    @pl.loop(0, EARLY)
    def _(j):
        late_copy(j).wait_recv()
        notes_copy(j).wait_recv()
        results = unit(
            [
                (raw_in[j, i], late_halo[j, i], notes_in[j, i : i + 1], notes_in[j, 2 + i : 3 + i])
                for i in range(2)
            ]
        )
        for i in range(2):
            valid = notes_in[j, 4 + i : 5 + i] > 0.5
            res = results[i]
            late_done[j, i] = jnp.where(valid, res, jnp.zeros_like(res)).astype(jnp.bfloat16)
        late_out(j).start()

    for d in range(1, TM):
        stat_copy(d, pos).wait_send()

    @pl.loop(0, PAIRS)
    def _(m):
        halo_copy(m).wait_send()

    @pl.loop(0, EARLY)
    def _(j):
        raw_copy(j).wait_send()
        late_copy(j).wait_send()
        notes_copy(j).wait_send()
        late_out(j).wait()

    own.wait()

    @pl.loop(0, SENDS)
    def _(i):
        out_copy(i).wait_send()

    @pl.loop(0, SENDS)
    def _(i):
        out_copy(i).wait_recv()


def on_device(tiles, buckets, tile_frames, norm_gain, norm_shift, conv_weight, conv_bias):
    hbm = pl.BlockSpec(memory_space=pltpu.HBM)
    any_ = pl.BlockSpec(memory_space=pl.ANY)
    bf16, f32 = jnp.bfloat16, jnp.float32
    out = pl.pallas_call(
        kernel,
        out_shape=jax.ShapeDtypeStruct((CLIP, 2, ROWS, CHANS), bf16),
        in_specs=[hbm] * 8,
        out_specs=any_,
        scratch_shapes=[
            pltpu.VMEM((TILES, ROWS, CHANS), bf16),
            pltpu.VMEM((1, TILES), jnp.int32),
            pltpu.VMEM((1, TILES), jnp.int32),
            pltpu.SMEM((TILES,), jnp.int32),
            pltpu.VMEM((1, CHANS), f32),
            pltpu.VMEM((1, CHANS), f32),
            pltpu.VMEM((1, CHANS), f32),
            pltpu.VMEM((PAIRS, 2, ROWS // 2, CHANS), bf16),
            pltpu.VMEM((PAIRS, 2, ROWS // 2, CHANS), bf16),
            pltpu.VMEM((TM, 2, TILES, CHANS), f32),
            pltpu.VMEM((TILES, CHANS), f32),
            pltpu.VMEM((TILES, CHANS), f32),
            pltpu.VMEM((3, 2, 6, 5, 16, CHANS), bf16),
            pltpu.VMEM((9, 4, CHANS, 2 * CHANS), bf16),
            pltpu.VMEM((TILES, ROWS, CHANS), bf16),
            pltpu.VMEM((SENDS + 1, 2, ROWS, CHANS), bf16),
            pltpu.VMEM((8, CHANS), jnp.int32),
            pltpu.SMEM((8, CHANS), jnp.int32),
            pltpu.VMEM((EARLY, 2, ROWS, CHANS), bf16),
            pltpu.VMEM((EARLY, 2, ROWS, CHANS), bf16),
            pltpu.VMEM((EARLY, 2, ROWS // 2, CHANS), bf16),
            pltpu.VMEM((EARLY, 2, ROWS, CHANS), bf16),
            pltpu.VMEM((EARLY, 8, CHANS), f32),
            pltpu.VMEM((EARLY, 8, CHANS), f32),
            pltpu.SemaphoreType.DMA((CHUNKS,)),
            pltpu.SemaphoreType.DMA((6,)),
            pltpu.SemaphoreType.DMA((18,)),
            pltpu.SemaphoreType.DMA((3,)),
            pltpu.SemaphoreType.DMA((PAIRS,)),
            pltpu.SemaphoreType.DMA((PAIRS,)),
            pltpu.SemaphoreType.DMA((TM,)),
            pltpu.SemaphoreType.DMA((TM,)),
            pltpu.SemaphoreType.DMA((SENDS,)),
            pltpu.SemaphoreType.DMA((SENDS,)),
            pltpu.SemaphoreType.DMA((EARLY,)),
            pltpu.SemaphoreType.DMA((EARLY,)),
            pltpu.SemaphoreType.DMA((EARLY,)),
            pltpu.SemaphoreType.DMA((EARLY,)),
            pltpu.SemaphoreType.DMA((EARLY,)),
            pltpu.SemaphoreType.DMA((EARLY,)),
            pltpu.SemaphoreType.DMA((EARLY,)),
        ],
        compiler_params=pltpu.CompilerParams(
            collective_id=0, has_side_effects=True, vmem_limit_bytes=40 << 20
        ),
        name="encode_and_send",
    )(
        *[
            pltpu.with_memory_space_constraint(v, pltpu.HBM)
            for v in (
                tiles.reshape(TILES, ROWS, CHANS),
                buckets.reshape(1, TILES),
                tile_frames.reshape(1, TILES),
                tile_frames,
                norm_gain.reshape(1, CHANS),
                norm_shift.reshape(1, CHANS),
                conv_weight,
                conv_bias.reshape(1, CHANS),
            )
        ]
    )
    return out.reshape((2 * CLIP,) + tiles.shape[1:])


def solution(mesh):
    in_specs = (P("clip", "tm", None, None, None), P("clip", None), P("clip"), P(), P(), P(), P())
    out_specs = P("clip", "tm", None, None, None)
    return jax.shard_map(
        on_device, mesh=mesh, in_specs=in_specs, out_specs=out_specs, check_vma=False
    )
```

```python
import jax
import jax.numpy as jnp
from jax import lax
from jax.experimental import pallas as pl
from jax.experimental.pallas import tpu as pltpu
from jax.sharding import PartitionSpec as P

MESH = pl.DeviceIdType.MESH
CLIP, TM = 32, 4
TILES, CELLS, CHANS = 32, 64, 128
ROWS = 4 * CELLS
PAIRS = TILES // 2
CHUNKS = 4
EARLY = 8
SENDS = CLIP - 1 - EARLY


SETS = [
    [(2, 3), (0, 1)],
    [(2, 2)],
    [(2, 1), (0, 3)],
    [(2, 0), (0, 2)],
    [(1, 2), (3, 0)],
    [(1, 3), (3, 1)],
    [(3, 2), (1, 0)],
    [(1, 1), (3, 3)],
]
ORDER = [(dx, dz, dc) for s in SETS for dc in range(2) for dx, dz in s] + [(0, 0, 1)]
assert sorted(ORDER) == [(x, z, c) for x in range(4) for z in range(4) for c in range(2)][1:]


def packed(values):
    return [sum(v << 2 * i for i, v in enumerate(values[h : h + 15])) for h in (0, 15, 30)]


WORDS = [packed([o[i] for o in ORDER]) for i in range(3)]


def here():
    me = lax.axis_index("clip")
    return lax.div(me, 8), lax.rem(lax.div(me, 2), 4), lax.rem(me, 2)


def offset(k):
    part, by = lax.div(k, 15), 2 * lax.rem(k, 15)
    words = [jnp.where(part == 0, w[0], jnp.where(part == 1, w[1], w[2])) for w in WORDS]
    return [lax.rem(lax.shift_right_logical(w, by), 4) for w in words]


def target(k):
    x, z, core = here()
    dx, dz, dc = offset(jnp.int32(k))
    return (lax.rem(x + dx, 4) * 4 + lax.rem(z + dz, 4)) * 2 + lax.rem(core + dc, 2)


def origin(k):
    x, z, core = here()
    dx, dz, dc = offset(jnp.int32(k))
    return (lax.rem(x + 4 - dx, 4) * 4 + lax.rem(z + 4 - dz, 4)) * 2 + lax.rem(core + 2 - dc, 2)


def place_of(group):
    x, z, core = here()
    step = jnp.full(group.shape, SENDS, jnp.int32)
    for k, (dx, dz, dc) in enumerate(ORDER):
        there = (lax.rem(x + dx, 4) * 4 + lax.rem(z + dz, 4)) * 2 + lax.rem(core + dc, 2)
        step = jnp.where(group == there, k - EARLY if k >= EARLY else SENDS + 1 + k, step)
    return step


def group_sum(v):
    lane = lax.broadcasted_iota(jnp.int32, v.shape, 1)
    for step in (1, 2):
        up = pltpu.roll(v, CHANS - step, 1)
        down = pltpu.roll(v, step, 1)
        v = v + jnp.where((lane // step) % 2 == 0, up, down)
    return v


def column_of(row):
    wide = jnp.broadcast_to(row, (TILES, TILES))
    r = lax.broadcasted_iota(jnp.int32, (TILES, TILES), 0)
    c = lax.broadcasted_iota(jnp.int32, (TILES, TILES), 1)
    return jnp.sum(jnp.where(r == c, wide, 0), axis=1, keepdims=True)


def kernel(
    x_hbm, bucket_hbm, frames_row_hbm, frames_hbm, gain_hbm, shift_hbm, w_hbm, bias_hbm, out_ref,
    x_s, bucket_s, frames_row, frames_smem, gain_ref, shift_ref, bias_ref,
    halo_out, halo_in, stats, mean_s, scale_s, acts, wide_w, done, send, table_v, table,
    raw_out, raw_in, late_halo, late_done, notes_out, notes_in,
    x_sem, small_sem, w_sem, local_sem, halo_ssem, halo_rsem, stat_ssem, stat_rsem, out_ssem, out_rsem,
    raw_ssem, raw_rsem, late_ssem, late_rsem, notes_ssem, notes_rsem, late_sem,
):
    me, pos = lax.axis_index("clip"), lax.axis_index("tm")

    smalls = [
        (bucket_hbm, bucket_s), (frames_row_hbm, frames_row), (frames_hbm, frames_smem),
        (gain_hbm, gain_ref), (shift_hbm, shift_ref), (bias_hbm, bias_ref),
    ]
    small_copies = [
        pltpu.make_async_copy(src, dst, small_sem.at[i]) for i, (src, dst) in enumerate(smalls)
    ]
    small_copies[0].start()
    x_copies = []
    for q in range(CHUNKS):
        part = pl.ds(q * (TILES // CHUNKS), TILES // CHUNKS)
        x_copies.append(pltpu.make_async_copy(x_hbm.at[part], x_s.at[part], x_sem.at[q]))
        x_copies[q].start()

    barrier = pltpu.get_barrier_semaphore()
    x, z, core = here()
    for dx, dz, dc in ORDER:
        there = (lax.rem(x + dx, 4) * 4 + lax.rem(z + dz, 4)) * 2 + lax.rem(core + dc, 2)
        pl.semaphore_signal(barrier, inc=1, device_id={"clip": there}, device_id_type=MESH)
    for d in range(1, TM):
        there = lax.rem(pos + d, TM)
        pl.semaphore_signal(barrier, inc=1, device_id={"tm": there}, device_id_type=MESH)

    for copy in small_copies[1:]:
        copy.start()
    w_copies = []
    for kt in range(3):
        for kw in range(3):
            for odd in range(2):
                copy = pltpu.make_async_copy(
                    w_hbm.at[kt, :, kw],
                    wide_w.at[kt * 3 + kw, pl.ds(odd, 3), :, pl.ds(odd * CHANS, CHANS)],
                    w_sem.at[(kt * 3 + kw) * 2 + odd],
                )
                copy.start()
                w_copies.append(copy)

    small_copies[0].wait()
    step_row = place_of(bucket_s[...])
    step_col = column_of(step_row)
    r = lax.broadcasted_iota(jnp.int32, (TILES, TILES), 0)
    c = lax.broadcasted_iota(jnp.int32, (TILES, TILES), 1)
    other = jnp.broadcast_to(step_row, (TILES, TILES))
    mine = jnp.broadcast_to(step_col, (TILES, TILES))
    ahead = jnp.where((other < mine) | ((other == mine) & (c < r)), 1, 0)
    place_col = jnp.sum(ahead, axis=1, keepdims=True)
    lanes = lax.broadcasted_iota(jnp.int32, (TILES, CHANS), 1)
    tiles_down = lax.broadcasted_iota(jnp.int32, (TILES, CHANS), 0)
    order = jnp.sum(jnp.where(place_col == lanes, tiles_down, 0), axis=0, keepdims=True)
    start = jnp.sum(jnp.where(step_col < lanes, 1, 0), axis=0, keepdims=True)
    table_v[...] = jnp.zeros_like(table_v)
    table_v[0:1, :] = order
    table_v[1:2, :] = start
    table_copy = pltpu.make_async_copy(table_v, table, local_sem.at[1])
    table_copy.start()

    zeros_w = jnp.zeros((9, CHANS, CHANS), jnp.bfloat16)
    wide_w[:, 3, :, 0:CHANS] = zeros_w
    wide_w[:, 0, :, CHANS : 2 * CHANS] = zeros_w
    pad = jnp.zeros((6, 16, CHANS), jnp.bfloat16)
    for kw in range(3):
        acts[kw, 0, :, 0] = pad
        acts[kw, 1, :, 4] = pad

    def raw_copy(j):
        return pltpu.make_async_remote_copy(
            src_ref=raw_out.at[j],
            dst_ref=raw_in.at[j],
            send_sem=raw_ssem.at[j],
            recv_sem=raw_rsem.at[j],
            device_id={"clip": target(j)},
            device_id_type=MESH,
        )

    def early_slots(j):
        first, after = table[1, CLIP - EARLY + j], table[1, CLIP - EARLY + 1 + j]
        places = [first, first + 1]
        return [(table[0, jnp.minimum(at, TILES - 1)], after > at) for at in places]

    table_copy.wait()
    for copy in x_copies:
        copy.wait()

    @pl.loop(0, EARLY)
    def _(j):
        for i, (t, _) in enumerate(early_slots(j)):
            raw_out[j, i] = x_s[t]

    pl.semaphore_wait(barrier, CLIP - 1 + TM - 1)

    @pl.loop(0, EARLY)
    def _(j):
        raw_copy(j).start()

    def stat_copy(d, there):
        return pltpu.make_async_remote_copy(
            src_ref=stats.at[pos],
            dst_ref=stats.at[there],
            send_sem=stat_ssem.at[d],
            recv_sem=stat_rsem.at[d],
            device_id={"tm": lax.rem(pos + d, TM)},
            device_id_type=MESH,
        )

    for q in range(CHUNKS):
        @pl.loop(q * (TILES // CHUNKS), (q + 1) * (TILES // CHUNKS), unroll=4)
        def _(t):
            xf = x_s[t].astype(jnp.float32)
            pivot = xf[0:1]
            dev = (xf - pivot).reshape(ROWS // 8, 8, CHANS)
            first = jnp.sum(jnp.sum(dev, axis=0), axis=0, keepdims=True) * (1.0 / ROWS)
            second = jnp.sum(jnp.sum(dev * dev, axis=0), axis=0, keepdims=True)
            stats[pos, 0, pl.ds(t, 1), :] = pivot + first
            stats[pos, 1, pl.ds(t, 1), :] = jnp.maximum(second - float(ROWS) * (first * first), 0.0)

    for d in range(1, TM):
        stat_copy(d, pos).start()

    def halo_copy(m):
        return pltpu.make_async_remote_copy(
            src_ref=halo_out.at[m],
            dst_ref=halo_in.at[m],
            send_sem=halo_ssem.at[m],
            recv_sem=halo_rsem.at[m],
            device_id={"tm": lax.rem(pos + 1, TM)},
            device_id_type=MESH,
        )

    @pl.loop(0, PAIRS)
    def _(m):
        for i in range(2):
            halo_out[m, i] = x_s[table[0, 2 * m + i], ROWS // 2 : ROWS, :]
        halo_copy(m).start()

    for copy in small_copies[1:]:
        copy.wait()
    for d in range(1, TM):
        stat_copy(d, lax.rem(pos + TM - d, TM)).wait_recv()

    length = column_of(frames_row[...])
    total = jnp.zeros((TILES, CHANS), jnp.float32)
    weights = [jnp.where(length > 4 * j, 1.0, 0.0) for j in range(TM)]
    parts = weights[0] + weights[1] + weights[2] + weights[3]
    for j in range(TM):
        total = total + stats[j, 0] * weights[j]
    mean = group_sum(total) / (parts * 4.0)
    spread = jnp.zeros((TILES, CHANS), jnp.float32)
    for j in range(TM):
        dev = stats[j, 0] - mean
        spread = spread + (stats[j, 1] + float(ROWS) * (dev * dev)) * weights[j]
    var = group_sum(spread) / (parts * (4.0 * ROWS))
    mean_s[...] = mean
    scale_s[...] = lax.rsqrt(var + 1e-06) * (0.5 * gain_ref[...])

    half_shift = 0.5 * shift_ref[...]
    bias = bias_ref[...]
    for copy in w_copies:
        copy.wait()

    def fill(i, slot, at, held):
        got = done[jnp.minimum(at, TILES - 1)]
        send[i, slot] = jnp.where(held, got, jnp.zeros_like(got))

    def out_copy(i):
        return pltpu.make_async_remote_copy(
            src_ref=send.at[i],
            dst_ref=out_ref.at[me],
            send_sem=out_ssem.at[i],
            recv_sem=out_rsem.at[i],
            device_id={"clip": target(i + EARLY)},
            device_id_type=MESH,
        )

    def fill_both(i):
        first, after = table[1, i], table[1, i + 1]
        fill(i, 0, first, after > first)
        fill(i, 1, first + 1, after > first + 1)

    def unit(tiles):
        series = []
        for cells, before, mean_t, scale_t in tiles:
            xb = cells.astype(jnp.float32).reshape(4, 8, 8, CHANS)
            hb = before.astype(jnp.float32).reshape(2, 8, 8, CHANS)
            hb = jnp.where(pos == 0, jnp.broadcast_to(xb[0:1], hb.shape), hb)
            raw = jnp.concatenate([hb, xb], axis=0)
            mean_t = mean_t.reshape(1, 1, 1, CHANS)
            scale_t = scale_t.reshape(1, 1, 1, CHANS)
            h = (raw - mean_t) * scale_t + half_shift.reshape(1, 1, 1, CHANS)
            series.append((h * jnp.tanh(h) + h).reshape(48, 8, CHANS))
        w = lax.broadcasted_iota(jnp.int32, (48, 8, CHANS), 1)
        for kw in range(3):
            moved = []
            for act in series:
                if kw == 0:
                    act = jnp.where(w == 0, 0.0, pltpu.roll(act, 1, 1))
                if kw == 2:
                    act = jnp.where(w == 7, 0.0, pltpu.roll(act, 7, 1))
                moved.append(act.reshape(6, 8, 1, 8, CHANS))
            both = jnp.concatenate(moved, axis=2).reshape(6, 4, 2, 16, CHANS).astype(jnp.bfloat16)
            acts[kw, 1, :, 0:4] = both[:, :, 0]
            acts[kw, 0, :, 1:5] = both[:, :, 1]
        cols = []
        for kt in range(3):
            for kw in range(3):
                for j in range(4):
                    part = acts[kw, j % 2, kt : kt + 4, j // 2 : j // 2 + 4]
                    cols.append(part.reshape(256, CHANS))
        conv = jnp.dot(
            jnp.concatenate(cols, axis=1),
            wide_w[...].reshape(36 * CHANS, 2 * CHANS),
            preferred_element_type=jnp.float32,
        )
        rows = [
            conv[:, 0:CHANS].reshape(4, 4, 2, 8, CHANS),
            conv[:, CHANS:].reshape(4, 4, 2, 8, CHANS),
        ]
        results = []
        for i, (cells, _, _, _) in enumerate(tiles):
            both = jnp.concatenate([v[:, :, i : i + 1] for v in rows], axis=2)
            results.append(cells.astype(jnp.float32) + both.reshape(ROWS, CHANS) + bias)
        return results

    def late_copy(j):
        return pltpu.make_async_remote_copy(
            src_ref=raw_in.at[j, :, pl.ds(ROWS // 2, ROWS // 2)],
            dst_ref=late_halo.at[j],
            send_sem=late_ssem.at[j],
            recv_sem=late_rsem.at[j],
            device_id={"tm": lax.rem(pos + 1, TM)},
            device_id_type=MESH,
        )

    def notes_copy(j):
        return pltpu.make_async_remote_copy(
            src_ref=notes_out.at[j],
            dst_ref=notes_in.at[j],
            send_sem=notes_ssem.at[j],
            recv_sem=notes_rsem.at[j],
            device_id={"clip": target(j)},
            device_id_type=MESH,
        )

    @pl.loop(0, EARLY)
    def _(j):
        notes_out[j] = jnp.zeros((8, CHANS), jnp.float32)
        for i, (t, held) in enumerate(early_slots(j)):
            notes_out[j, i : i + 1] = mean_s[pl.ds(t, 1), :]
            notes_out[j, 2 + i : 3 + i] = scale_s[pl.ds(t, 1), :]
            valid = held & (frames_smem[t] > 4 * pos)
            notes_out[j, 4 + i : 5 + i] = jnp.where(valid, jnp.ones((1, CHANS)), jnp.zeros((1, CHANS)))
        notes_copy(j).start()

    @pl.loop(0, PAIRS)
    def _(m):
        halo_copy(m).wait_recv()
        tiles = [table[0, 2 * m + i] for i in range(2)]
        results = unit(
            [
                (x_s[t], halo_in[m, i], mean_s[pl.ds(t, 1), :], scale_s[pl.ds(t, 1), :])
                for i, t in enumerate(tiles)
            ]
        )
        for i, t in enumerate(tiles):
            valid = frames_smem[t] > 4 * pos
            res = results[i]
            done[2 * m + i] = jnp.where(valid, res, jnp.zeros_like(res)).astype(jnp.bfloat16)
        fill_both(m)
        out_copy(m).start()

        @pl.when(m >= PAIRS - EARLY)
        def _():
            raw_copy(m - (PAIRS - EARLY)).wait_recv()
            late_copy(m - (PAIRS - EARLY)).start()

    @pl.loop(PAIRS, SENDS)
    def _(i):
        fill_both(i)
        out_copy(i).start()

    fill_both(SENDS)
    own = pltpu.make_async_copy(send.at[SENDS], out_ref.at[me], local_sem.at[2])
    own.start()

    def late_out(j):
        return pltpu.make_async_copy(late_done.at[j], out_ref.at[origin(j)], late_sem.at[j])

    @pl.loop(0, EARLY)
    def _(j):
        late_copy(j).wait_recv()
        notes_copy(j).wait_recv()
        results = unit(
            [
                (raw_in[j, i], late_halo[j, i], notes_in[j, i : i + 1], notes_in[j, 2 + i : 3 + i])
                for i in range(2)
            ]
        )
        for i in range(2):
            valid = notes_in[j, 4 + i : 5 + i] > 0.5
            res = results[i]
            late_done[j, i] = jnp.where(valid, res, jnp.zeros_like(res)).astype(jnp.bfloat16)
        late_out(j).start()

    for d in range(1, TM):
        stat_copy(d, pos).wait_send()

    @pl.loop(0, PAIRS)
    def _(m):
        halo_copy(m).wait_send()

    @pl.loop(0, EARLY)
    def _(j):
        raw_copy(j).wait_send()
        late_copy(j).wait_send()
        notes_copy(j).wait_send()
        late_out(j).wait()

    own.wait()

    @pl.loop(0, SENDS)
    def _(i):
        out_copy(i).wait_send()

    @pl.loop(0, SENDS)
    def _(i):
        out_copy(i).wait_recv()


def on_device(tiles, buckets, tile_frames, norm_gain, norm_shift, conv_weight, conv_bias):
    hbm = pl.BlockSpec(memory_space=pltpu.HBM)
    any_ = pl.BlockSpec(memory_space=pl.ANY)
    bf16, f32 = jnp.bfloat16, jnp.float32
    out = pl.pallas_call(
        kernel,
        out_shape=jax.ShapeDtypeStruct((CLIP, 2, ROWS, CHANS), bf16),
        in_specs=[hbm] * 8,
        out_specs=any_,
        scratch_shapes=[
            pltpu.VMEM((TILES, ROWS, CHANS), bf16),
            pltpu.VMEM((1, TILES), jnp.int32),
            pltpu.VMEM((1, TILES), jnp.int32),
            pltpu.SMEM((TILES,), jnp.int32),
            pltpu.VMEM((1, CHANS), f32),
            pltpu.VMEM((1, CHANS), f32),
            pltpu.VMEM((1, CHANS), f32),
            pltpu.VMEM((PAIRS, 2, ROWS // 2, CHANS), bf16),
            pltpu.VMEM((PAIRS, 2, ROWS // 2, CHANS), bf16),
            pltpu.VMEM((TM, 2, TILES, CHANS), f32),
            pltpu.VMEM((TILES, CHANS), f32),
            pltpu.VMEM((TILES, CHANS), f32),
            pltpu.VMEM((3, 2, 6, 5, 16, CHANS), bf16),
            pltpu.VMEM((9, 4, CHANS, 2 * CHANS), bf16),
            pltpu.VMEM((TILES, ROWS, CHANS), bf16),
            pltpu.VMEM((SENDS + 1, 2, ROWS, CHANS), bf16),
            pltpu.VMEM((8, CHANS), jnp.int32),
            pltpu.SMEM((8, CHANS), jnp.int32),
            pltpu.VMEM((EARLY, 2, ROWS, CHANS), bf16),
            pltpu.VMEM((EARLY, 2, ROWS, CHANS), bf16),
            pltpu.VMEM((EARLY, 2, ROWS // 2, CHANS), bf16),
            pltpu.VMEM((EARLY, 2, ROWS, CHANS), bf16),
            pltpu.VMEM((EARLY, 8, CHANS), f32),
            pltpu.VMEM((EARLY, 8, CHANS), f32),
            pltpu.SemaphoreType.DMA((CHUNKS,)),
            pltpu.SemaphoreType.DMA((6,)),
            pltpu.SemaphoreType.DMA((18,)),
            pltpu.SemaphoreType.DMA((3,)),
            pltpu.SemaphoreType.DMA((PAIRS,)),
            pltpu.SemaphoreType.DMA((PAIRS,)),
            pltpu.SemaphoreType.DMA((TM,)),
            pltpu.SemaphoreType.DMA((TM,)),
            pltpu.SemaphoreType.DMA((SENDS,)),
            pltpu.SemaphoreType.DMA((SENDS,)),
            pltpu.SemaphoreType.DMA((EARLY,)),
            pltpu.SemaphoreType.DMA((EARLY,)),
            pltpu.SemaphoreType.DMA((EARLY,)),
            pltpu.SemaphoreType.DMA((EARLY,)),
            pltpu.SemaphoreType.DMA((EARLY,)),
            pltpu.SemaphoreType.DMA((EARLY,)),
            pltpu.SemaphoreType.DMA((EARLY,)),
        ],
        compiler_params=pltpu.CompilerParams(
            collective_id=0, has_side_effects=True, vmem_limit_bytes=40 << 20
        ),
        name="encode_and_send",
    )(
        *[
            pltpu.with_memory_space_constraint(v, pltpu.HBM)
            for v in (
                tiles.reshape(TILES, ROWS, CHANS),
                buckets.reshape(1, TILES),
                tile_frames.reshape(1, TILES),
                tile_frames,
                norm_gain.reshape(1, CHANS),
                norm_shift.reshape(1, CHANS),
                conv_weight,
                conv_bias.reshape(1, CHANS),
            )
        ]
    )
    return out.reshape((2 * CLIP,) + tiles.shape[1:])


def solution(mesh):
    in_specs = (P("clip", "tm", None, None, None), P("clip", None), P("clip"), P(), P(), P(), P())
    out_specs = P("clip", "tm", None, None, None)
    return jax.shard_map(
        on_device, mesh=mesh, in_specs=in_specs, out_specs=out_specs, check_vma=False
    )
```

```python
import jax
import jax.numpy as jnp
from jax import lax
from jax.experimental import pallas as pl
from jax.experimental.pallas import tpu as pltpu
from jax.sharding import PartitionSpec as P

MESH = pl.DeviceIdType.MESH
CLIP, TM = 32, 4
TILES, CELLS, CHANS = 32, 64, 128
ROWS = 4 * CELLS
PAIRS = TILES // 2
CHUNKS = 4
EARLY = 8
SENDS = CLIP - 1 - EARLY


SETS = [
    [(2, 3), (0, 1)],
    [(2, 2)],
    [(2, 1), (0, 3)],
    [(2, 0), (0, 2)],
    [(1, 2), (3, 0)],
    [(1, 3), (3, 1)],
    [(3, 2), (1, 0)],
    [(1, 1), (3, 3)],
]
ORDER = [(dx, dz, dc) for s in SETS for dc in range(2) for dx, dz in s] + [(0, 0, 1)]
assert sorted(ORDER) == [(x, z, c) for x in range(4) for z in range(4) for c in range(2)][1:]


def packed(values):
    return [sum(v << 2 * i for i, v in enumerate(values[h : h + 15])) for h in (0, 15, 30)]


WORDS = [packed([o[i] for o in ORDER]) for i in range(3)]


def here():
    me = lax.axis_index("clip")
    return lax.div(me, 8), lax.rem(lax.div(me, 2), 4), lax.rem(me, 2)


def offset(k):
    part, by = lax.div(k, 15), 2 * lax.rem(k, 15)
    words = [jnp.where(part == 0, w[0], jnp.where(part == 1, w[1], w[2])) for w in WORDS]
    return [lax.rem(lax.shift_right_logical(w, by), 4) for w in words]


def target(k):
    x, z, core = here()
    dx, dz, dc = offset(jnp.int32(k))
    return (lax.rem(x + dx, 4) * 4 + lax.rem(z + dz, 4)) * 2 + lax.rem(core + dc, 2)


def origin(k):
    x, z, core = here()
    dx, dz, dc = offset(jnp.int32(k))
    return (lax.rem(x + 4 - dx, 4) * 4 + lax.rem(z + 4 - dz, 4)) * 2 + lax.rem(core + 2 - dc, 2)


def place_of(group):
    x, z, core = here()
    step = jnp.full(group.shape, SENDS, jnp.int32)
    for k, (dx, dz, dc) in enumerate(ORDER):
        there = (lax.rem(x + dx, 4) * 4 + lax.rem(z + dz, 4)) * 2 + lax.rem(core + dc, 2)
        step = jnp.where(group == there, k - EARLY if k >= EARLY else SENDS + 1 + k, step)
    return step


def group_sum(v):
    lane = lax.broadcasted_iota(jnp.int32, v.shape, 1)
    for step in (1, 2):
        up = pltpu.roll(v, CHANS - step, 1)
        down = pltpu.roll(v, step, 1)
        v = v + jnp.where((lane // step) % 2 == 0, up, down)
    return v


def column_of(row):
    wide = jnp.broadcast_to(row, (TILES, TILES))
    r = lax.broadcasted_iota(jnp.int32, (TILES, TILES), 0)
    c = lax.broadcasted_iota(jnp.int32, (TILES, TILES), 1)
    return jnp.sum(jnp.where(r == c, wide, 0), axis=1, keepdims=True)


def kernel(
    x_hbm, bucket_hbm, frames_row_hbm, frames_hbm, gain_hbm, shift_hbm, w_hbm, bias_hbm, out_ref,
    x_s, bucket_s, frames_row, frames_smem, gain_ref, shift_ref, bias_ref,
    halo_out, halo_in, stats, mean_s, scale_s, acts, wide_w, done, send, table_v, table,
    raw_out, raw_in, late_halo, late_done, notes_out, notes_in,
    x_sem, small_sem, w_sem, local_sem, halo_ssem, halo_rsem, stat_ssem, stat_rsem, out_ssem, out_rsem,
    raw_ssem, raw_rsem, late_ssem, late_rsem, notes_ssem, notes_rsem, late_sem,
):
    me, pos = lax.axis_index("clip"), lax.axis_index("tm")

    smalls = [
        (bucket_hbm, bucket_s), (frames_row_hbm, frames_row), (frames_hbm, frames_smem),
        (gain_hbm, gain_ref), (shift_hbm, shift_ref), (bias_hbm, bias_ref),
    ]
    small_copies = [
        pltpu.make_async_copy(src, dst, small_sem.at[i]) for i, (src, dst) in enumerate(smalls)
    ]
    small_copies[0].start()
    x_copies = []
    for q in range(CHUNKS):
        part = pl.ds(q * (TILES // CHUNKS), TILES // CHUNKS)
        x_copies.append(pltpu.make_async_copy(x_hbm.at[part], x_s.at[part], x_sem.at[q]))
        x_copies[q].start()

    barrier = pltpu.get_barrier_semaphore()
    x, z, core = here()
    for dx, dz, dc in ORDER:
        there = (lax.rem(x + dx, 4) * 4 + lax.rem(z + dz, 4)) * 2 + lax.rem(core + dc, 2)
        pl.semaphore_signal(barrier, inc=1, device_id={"clip": there}, device_id_type=MESH)
    for d in range(1, TM):
        there = lax.rem(pos + d, TM)
        pl.semaphore_signal(barrier, inc=1, device_id={"tm": there}, device_id_type=MESH)

    for copy in small_copies[1:]:
        copy.start()
    w_copies = []
    for kt in range(3):
        for kw in range(3):
            for odd in range(2):
                copy = pltpu.make_async_copy(
                    w_hbm.at[kt, :, kw],
                    wide_w.at[kt * 3 + kw, pl.ds(odd, 3), :, pl.ds(odd * CHANS, CHANS)],
                    w_sem.at[(kt * 3 + kw) * 2 + odd],
                )
                copy.start()
                w_copies.append(copy)

    small_copies[0].wait()
    step_row = place_of(bucket_s[...])
    step_col = column_of(step_row)
    r = lax.broadcasted_iota(jnp.int32, (TILES, TILES), 0)
    c = lax.broadcasted_iota(jnp.int32, (TILES, TILES), 1)
    other = jnp.broadcast_to(step_row, (TILES, TILES))
    mine = jnp.broadcast_to(step_col, (TILES, TILES))
    ahead = jnp.where((other < mine) | ((other == mine) & (c < r)), 1, 0)
    place_col = jnp.sum(ahead, axis=1, keepdims=True)
    lanes = lax.broadcasted_iota(jnp.int32, (TILES, CHANS), 1)
    tiles_down = lax.broadcasted_iota(jnp.int32, (TILES, CHANS), 0)
    order = jnp.sum(jnp.where(place_col == lanes, tiles_down, 0), axis=0, keepdims=True)
    start = jnp.sum(jnp.where(step_col < lanes, 1, 0), axis=0, keepdims=True)
    table_v[...] = jnp.zeros_like(table_v)
    table_v[0:1, :] = order
    table_v[1:2, :] = start
    table_copy = pltpu.make_async_copy(table_v, table, local_sem.at[1])
    table_copy.start()

    zeros_w = jnp.zeros((9, CHANS, CHANS), jnp.bfloat16)
    wide_w[:, 3, :, 0:CHANS] = zeros_w
    wide_w[:, 0, :, CHANS : 2 * CHANS] = zeros_w
    pad = jnp.zeros((6, 16, CHANS), jnp.bfloat16)
    for kw in range(3):
        acts[kw, 0, :, 0] = pad
        acts[kw, 1, :, 4] = pad

    def raw_copy(j):
        return pltpu.make_async_remote_copy(
            src_ref=raw_out.at[j],
            dst_ref=raw_in.at[j],
            send_sem=raw_ssem.at[j],
            recv_sem=raw_rsem.at[j],
            device_id={"clip": target(j)},
            device_id_type=MESH,
        )

    def early_slots(j):
        first, after = table[1, CLIP - EARLY + j], table[1, CLIP - EARLY + 1 + j]
        places = [first, first + 1]
        return [(table[0, jnp.minimum(at, TILES - 1)], after > at) for at in places]

    table_copy.wait()
    for copy in x_copies:
        copy.wait()

    @pl.loop(0, EARLY)
    def _(j):
        for i, (t, _) in enumerate(early_slots(j)):
            raw_out[j, i] = x_s[t]

    pl.semaphore_wait(barrier, CLIP - 1 + TM - 1)

    @pl.loop(0, EARLY)
    def _(j):
        raw_copy(j).start()

    def stat_copy(d, there):
        return pltpu.make_async_remote_copy(
            src_ref=stats.at[pos],
            dst_ref=stats.at[there],
            send_sem=stat_ssem.at[d],
            recv_sem=stat_rsem.at[d],
            device_id={"tm": lax.rem(pos + d, TM)},
            device_id_type=MESH,
        )

    for q in range(CHUNKS):
        @pl.loop(q * (TILES // CHUNKS), (q + 1) * (TILES // CHUNKS), unroll=4)
        def _(t):
            xf = x_s[t].astype(jnp.float32)
            pivot = xf[0:1]
            dev = (xf - pivot).reshape(ROWS // 8, 8, CHANS)
            first = jnp.sum(jnp.sum(dev, axis=0), axis=0, keepdims=True) * (1.0 / ROWS)
            second = jnp.sum(jnp.sum(dev * dev, axis=0), axis=0, keepdims=True)
            stats[pos, 0, pl.ds(t, 1), :] = pivot + first
            stats[pos, 1, pl.ds(t, 1), :] = jnp.maximum(second - float(ROWS) * (first * first), 0.0)

    for d in range(1, TM):
        stat_copy(d, pos).start()

    def halo_copy(m):
        return pltpu.make_async_remote_copy(
            src_ref=halo_out.at[m],
            dst_ref=halo_in.at[m],
            send_sem=halo_ssem.at[m],
            recv_sem=halo_rsem.at[m],
            device_id={"tm": lax.rem(pos + 1, TM)},
            device_id_type=MESH,
        )

    @pl.loop(0, PAIRS)
    def _(m):
        for i in range(2):
            halo_out[m, i] = x_s[table[0, 2 * m + i], ROWS // 2 : ROWS, :]

        @pl.when(pos < TM - 1)
        def _():
            halo_copy(m).start()


    for copy in small_copies[1:]:
        copy.wait()
    for d in range(1, TM):
        stat_copy(d, lax.rem(pos + TM - d, TM)).wait_recv()

    length = column_of(frames_row[...])
    total = jnp.zeros((TILES, CHANS), jnp.float32)
    weights = [jnp.where(length > 4 * j, 1.0, 0.0) for j in range(TM)]
    parts = weights[0] + weights[1] + weights[2] + weights[3]
    for j in range(TM):
        total = total + stats[j, 0] * weights[j]
    mean = group_sum(total) / (parts * 4.0)
    spread = jnp.zeros((TILES, CHANS), jnp.float32)
    for j in range(TM):
        dev = stats[j, 0] - mean
        spread = spread + (stats[j, 1] + float(ROWS) * (dev * dev)) * weights[j]
    var = group_sum(spread) / (parts * (4.0 * ROWS))
    mean_s[...] = mean
    scale_s[...] = lax.rsqrt(var + 1e-06) * (0.5 * gain_ref[...])

    half_shift = 0.5 * shift_ref[...]
    bias = bias_ref[...]
    for copy in w_copies:
        copy.wait()

    def fill(i, slot, at, held):
        got = done[jnp.minimum(at, TILES - 1)]
        send[i, slot] = jnp.where(held, got, jnp.zeros_like(got))

    def out_copy(i):
        return pltpu.make_async_remote_copy(
            src_ref=send.at[i],
            dst_ref=out_ref.at[me],
            send_sem=out_ssem.at[i],
            recv_sem=out_rsem.at[i],
            device_id={"clip": target(i + EARLY)},
            device_id_type=MESH,
        )

    def fill_both(i):
        first, after = table[1, i], table[1, i + 1]
        fill(i, 0, first, after > first)
        fill(i, 1, first + 1, after > first + 1)

    def unit(tiles):
        series = []
        for cells, before, mean_t, scale_t in tiles:
            xb = cells.astype(jnp.float32).reshape(4, 8, 8, CHANS)
            hb = before.astype(jnp.float32).reshape(2, 8, 8, CHANS)
            hb = jnp.where(pos == 0, jnp.broadcast_to(xb[0:1], hb.shape), hb)
            raw = jnp.concatenate([hb, xb], axis=0)
            mean_t = mean_t.reshape(1, 1, 1, CHANS)
            scale_t = scale_t.reshape(1, 1, 1, CHANS)
            h = (raw - mean_t) * scale_t + half_shift.reshape(1, 1, 1, CHANS)
            series.append((h * jnp.tanh(h) + h).reshape(48, 8, CHANS))
        w = lax.broadcasted_iota(jnp.int32, (48, 8, CHANS), 1)
        for kw in range(3):
            moved = []
            for act in series:
                if kw == 0:
                    act = jnp.where(w == 0, 0.0, pltpu.roll(act, 1, 1))
                if kw == 2:
                    act = jnp.where(w == 7, 0.0, pltpu.roll(act, 7, 1))
                moved.append(act.reshape(6, 8, 1, 8, CHANS))
            both = jnp.concatenate(moved, axis=2).reshape(6, 4, 2, 16, CHANS).astype(jnp.bfloat16)
            acts[kw, 1, :, 0:4] = both[:, :, 0]
            acts[kw, 0, :, 1:5] = both[:, :, 1]
        cols = []
        for kt in range(3):
            for kw in range(3):
                for j in range(4):
                    part = acts[kw, j % 2, kt : kt + 4, j // 2 : j // 2 + 4]
                    cols.append(part.reshape(256, CHANS))
        conv = jnp.dot(
            jnp.concatenate(cols, axis=1),
            wide_w[...].reshape(36 * CHANS, 2 * CHANS),
            preferred_element_type=jnp.float32,
        )
        rows = [
            conv[:, 0:CHANS].reshape(4, 4, 2, 8, CHANS),
            conv[:, CHANS:].reshape(4, 4, 2, 8, CHANS),
        ]
        results = []
        for i, (cells, _, _, _) in enumerate(tiles):
            both = jnp.concatenate([v[:, :, i : i + 1] for v in rows], axis=2)
            results.append(cells.astype(jnp.float32) + both.reshape(ROWS, CHANS) + bias)
        return results

    def late_copy(j):
        return pltpu.make_async_remote_copy(
            src_ref=raw_in.at[j, :, pl.ds(ROWS // 2, ROWS // 2)],
            dst_ref=late_halo.at[j],
            send_sem=late_ssem.at[j],
            recv_sem=late_rsem.at[j],
            device_id={"tm": lax.rem(pos + 1, TM)},
            device_id_type=MESH,
        )

    def notes_copy(j):
        return pltpu.make_async_remote_copy(
            src_ref=notes_out.at[j],
            dst_ref=notes_in.at[j],
            send_sem=notes_ssem.at[j],
            recv_sem=notes_rsem.at[j],
            device_id={"clip": target(j)},
            device_id_type=MESH,
        )

    @pl.loop(0, EARLY)
    def _(j):
        notes_out[j] = jnp.zeros((8, CHANS), jnp.float32)
        for i, (t, held) in enumerate(early_slots(j)):
            notes_out[j, i : i + 1] = mean_s[pl.ds(t, 1), :]
            notes_out[j, 2 + i : 3 + i] = scale_s[pl.ds(t, 1), :]
            valid = held & (frames_smem[t] > 4 * pos)
            notes_out[j, 4 + i : 5 + i] = jnp.where(valid, jnp.ones((1, CHANS)), jnp.zeros((1, CHANS)))
        notes_copy(j).start()

    @pl.loop(0, PAIRS)
    def _(m):

        @pl.when(pos > 0)
        def _():
            halo_copy(m).wait_recv()

        tiles = [table[0, 2 * m + i] for i in range(2)]
        results = unit(
            [
                (x_s[t], halo_in[m, i], mean_s[pl.ds(t, 1), :], scale_s[pl.ds(t, 1), :])
                for i, t in enumerate(tiles)
            ]
        )
        for i, t in enumerate(tiles):
            valid = frames_smem[t] > 4 * pos
            res = results[i]
            done[2 * m + i] = jnp.where(valid, res, jnp.zeros_like(res)).astype(jnp.bfloat16)
        fill_both(m)
        out_copy(m).start()

        @pl.when(m >= PAIRS - EARLY)
        def _():
            raw_copy(m - (PAIRS - EARLY)).wait_recv()

            @pl.when(pos < TM - 1)
            def _():
                late_copy(m - (PAIRS - EARLY)).start()


    @pl.loop(PAIRS, SENDS)
    def _(i):
        fill_both(i)
        out_copy(i).start()

    fill_both(SENDS)
    own = pltpu.make_async_copy(send.at[SENDS], out_ref.at[me], local_sem.at[2])
    own.start()

    def late_out(j):
        return pltpu.make_async_copy(late_done.at[j], out_ref.at[origin(j)], late_sem.at[j])

    @pl.loop(0, EARLY)
    def _(j):

        @pl.when(pos > 0)
        def _():
            late_copy(j).wait_recv()

        notes_copy(j).wait_recv()
        results = unit(
            [
                (raw_in[j, i], late_halo[j, i], notes_in[j, i : i + 1], notes_in[j, 2 + i : 3 + i])
                for i in range(2)
            ]
        )
        for i in range(2):
            valid = notes_in[j, 4 + i : 5 + i] > 0.5
            res = results[i]
            late_done[j, i] = jnp.where(valid, res, jnp.zeros_like(res)).astype(jnp.bfloat16)
        late_out(j).start()

    for d in range(1, TM):
        stat_copy(d, pos).wait_send()

    @pl.loop(0, PAIRS)
    def _(m):

        @pl.when(pos < TM - 1)
        def _():
            halo_copy(m).wait_send()


    @pl.loop(0, EARLY)
    def _(j):
        raw_copy(j).wait_send()

        @pl.when(pos < TM - 1)
        def _():
            late_copy(j).wait_send()

        notes_copy(j).wait_send()
        late_out(j).wait()

    own.wait()

    @pl.loop(0, SENDS)
    def _(i):
        out_copy(i).wait_send()

    @pl.loop(0, SENDS)
    def _(i):
        out_copy(i).wait_recv()


def on_device(tiles, buckets, tile_frames, norm_gain, norm_shift, conv_weight, conv_bias):
    hbm = pl.BlockSpec(memory_space=pltpu.HBM)
    any_ = pl.BlockSpec(memory_space=pl.ANY)
    bf16, f32 = jnp.bfloat16, jnp.float32
    out = pl.pallas_call(
        kernel,
        out_shape=jax.ShapeDtypeStruct((CLIP, 2, ROWS, CHANS), bf16),
        in_specs=[hbm] * 8,
        out_specs=any_,
        scratch_shapes=[
            pltpu.VMEM((TILES, ROWS, CHANS), bf16),
            pltpu.VMEM((1, TILES), jnp.int32),
            pltpu.VMEM((1, TILES), jnp.int32),
            pltpu.SMEM((TILES,), jnp.int32),
            pltpu.VMEM((1, CHANS), f32),
            pltpu.VMEM((1, CHANS), f32),
            pltpu.VMEM((1, CHANS), f32),
            pltpu.VMEM((PAIRS, 2, ROWS // 2, CHANS), bf16),
            pltpu.VMEM((PAIRS, 2, ROWS // 2, CHANS), bf16),
            pltpu.VMEM((TM, 2, TILES, CHANS), f32),
            pltpu.VMEM((TILES, CHANS), f32),
            pltpu.VMEM((TILES, CHANS), f32),
            pltpu.VMEM((3, 2, 6, 5, 16, CHANS), bf16),
            pltpu.VMEM((9, 4, CHANS, 2 * CHANS), bf16),
            pltpu.VMEM((TILES, ROWS, CHANS), bf16),
            pltpu.VMEM((SENDS + 1, 2, ROWS, CHANS), bf16),
            pltpu.VMEM((8, CHANS), jnp.int32),
            pltpu.SMEM((8, CHANS), jnp.int32),
            pltpu.VMEM((EARLY, 2, ROWS, CHANS), bf16),
            pltpu.VMEM((EARLY, 2, ROWS, CHANS), bf16),
            pltpu.VMEM((EARLY, 2, ROWS // 2, CHANS), bf16),
            pltpu.VMEM((EARLY, 2, ROWS, CHANS), bf16),
            pltpu.VMEM((EARLY, 8, CHANS), f32),
            pltpu.VMEM((EARLY, 8, CHANS), f32),
            pltpu.SemaphoreType.DMA((CHUNKS,)),
            pltpu.SemaphoreType.DMA((6,)),
            pltpu.SemaphoreType.DMA((18,)),
            pltpu.SemaphoreType.DMA((3,)),
            pltpu.SemaphoreType.DMA((PAIRS,)),
            pltpu.SemaphoreType.DMA((PAIRS,)),
            pltpu.SemaphoreType.DMA((TM,)),
            pltpu.SemaphoreType.DMA((TM,)),
            pltpu.SemaphoreType.DMA((SENDS,)),
            pltpu.SemaphoreType.DMA((SENDS,)),
            pltpu.SemaphoreType.DMA((EARLY,)),
            pltpu.SemaphoreType.DMA((EARLY,)),
            pltpu.SemaphoreType.DMA((EARLY,)),
            pltpu.SemaphoreType.DMA((EARLY,)),
            pltpu.SemaphoreType.DMA((EARLY,)),
            pltpu.SemaphoreType.DMA((EARLY,)),
            pltpu.SemaphoreType.DMA((EARLY,)),
        ],
        compiler_params=pltpu.CompilerParams(
            collective_id=0, has_side_effects=True, vmem_limit_bytes=40 << 20
        ),
        name="encode_and_send",
    )(
        *[
            pltpu.with_memory_space_constraint(v, pltpu.HBM)
            for v in (
                tiles.reshape(TILES, ROWS, CHANS),
                buckets.reshape(1, TILES),
                tile_frames.reshape(1, TILES),
                tile_frames,
                norm_gain.reshape(1, CHANS),
                norm_shift.reshape(1, CHANS),
                conv_weight,
                conv_bias.reshape(1, CHANS),
            )
        ]
    )
    return out.reshape((2 * CLIP,) + tiles.shape[1:])


def solution(mesh):
    in_specs = (P("clip", "tm", None, None, None), P("clip", None), P("clip"), P(), P(), P(), P())
    out_specs = P("clip", "tm", None, None, None)
    return jax.shard_map(
        on_device, mesh=mesh, in_specs=in_specs, out_specs=out_specs, check_vma=False
    )
```

```python
import jax
import jax.numpy as jnp
from jax import lax
from jax.experimental import pallas as pl
from jax.experimental.pallas import tpu as pltpu
from jax.sharding import PartitionSpec as P

MESH = pl.DeviceIdType.MESH
CLIP, TM = 32, 4
TILES, CELLS, CHANS = 32, 64, 128
ROWS = 4 * CELLS
PAIRS = TILES // 2
CHUNKS = 4
EARLY = 8
SENDS = CLIP - 1 - EARLY


SETS = [
    [(2, 3), (0, 1)],
    [(2, 2)],
    [(2, 1), (0, 3)],
    [(2, 0), (0, 2)],
    [(1, 2), (3, 0)],
    [(1, 3), (3, 1)],
    [(3, 2), (1, 0)],
    [(1, 1), (3, 3)],
]
ORDER = [(dx, dz, dc) for s in SETS for dc in range(2) for dx, dz in s] + [(0, 0, 1)]
assert sorted(ORDER) == [(x, z, c) for x in range(4) for z in range(4) for c in range(2)][1:]


def packed(values):
    return [sum(v << 2 * i for i, v in enumerate(values[h : h + 15])) for h in (0, 15, 30)]


WORDS = [packed([o[i] for o in ORDER]) for i in range(3)]


def here():
    me = lax.axis_index("clip")
    return lax.div(me, 8), lax.rem(lax.div(me, 2), 4), lax.rem(me, 2)


def offset(k):
    part, by = lax.div(k, 15), 2 * lax.rem(k, 15)
    words = [jnp.where(part == 0, w[0], jnp.where(part == 1, w[1], w[2])) for w in WORDS]
    return [lax.rem(lax.shift_right_logical(w, by), 4) for w in words]


def target(k):
    x, z, core = here()
    dx, dz, dc = offset(jnp.int32(k))
    return (lax.rem(x + dx, 4) * 4 + lax.rem(z + dz, 4)) * 2 + lax.rem(core + dc, 2)


def origin(k):
    x, z, core = here()
    dx, dz, dc = offset(jnp.int32(k))
    return (lax.rem(x + 4 - dx, 4) * 4 + lax.rem(z + 4 - dz, 4)) * 2 + lax.rem(core + 2 - dc, 2)


def place_of(group):
    x, z, core = here()
    step = jnp.full(group.shape, SENDS, jnp.int32)
    for k, (dx, dz, dc) in enumerate(ORDER):
        there = (lax.rem(x + dx, 4) * 4 + lax.rem(z + dz, 4)) * 2 + lax.rem(core + dc, 2)
        step = jnp.where(group == there, k - EARLY if k >= EARLY else SENDS + 1 + k, step)
    return step


def group_sum(v):
    lane = lax.broadcasted_iota(jnp.int32, v.shape, 1)
    for step in (1, 2):
        up = pltpu.roll(v, CHANS - step, 1)
        down = pltpu.roll(v, step, 1)
        v = v + jnp.where((lane // step) % 2 == 0, up, down)
    return v


def column_of(row):
    wide = jnp.broadcast_to(row, (TILES, TILES))
    r = lax.broadcasted_iota(jnp.int32, (TILES, TILES), 0)
    c = lax.broadcasted_iota(jnp.int32, (TILES, TILES), 1)
    return jnp.sum(jnp.where(r == c, wide, 0), axis=1, keepdims=True)


def kernel(
    x_hbm, bucket_hbm, frames_row_hbm, frames_hbm, gain_hbm, shift_hbm, w_hbm, bias_hbm, out_ref,
    x_s, bucket_s, frames_row, frames_smem, gain_ref, shift_ref, bias_ref,
    halo_out, halo_in, stats, mean_s, scale_s, acts, wide_w, done, send, table_v, table,
    raw_out, raw_in, late_halo, late_done, notes_out, notes_in,
    x_sem, small_sem, w_sem, local_sem, halo_ssem, halo_rsem, stat_ssem, stat_rsem, out_ssem, out_rsem,
    raw_ssem, raw_rsem, late_ssem, late_rsem, notes_ssem, notes_rsem, late_sem,
):
    me, pos = lax.axis_index("clip"), lax.axis_index("tm")

    smalls = [
        (bucket_hbm, bucket_s), (frames_row_hbm, frames_row), (frames_hbm, frames_smem),
        (gain_hbm, gain_ref), (shift_hbm, shift_ref), (bias_hbm, bias_ref),
    ]
    small_copies = [
        pltpu.make_async_copy(src, dst, small_sem.at[i]) for i, (src, dst) in enumerate(smalls)
    ]
    small_copies[0].start()
    x_copies = []
    for q in range(CHUNKS):
        part = pl.ds(q * (TILES // CHUNKS), TILES // CHUNKS)
        x_copies.append(pltpu.make_async_copy(x_hbm.at[part], x_s.at[part], x_sem.at[q]))
        x_copies[q].start()

    barrier = pltpu.get_barrier_semaphore()
    x, z, core = here()
    for dx, dz, dc in ORDER:
        there = (lax.rem(x + dx, 4) * 4 + lax.rem(z + dz, 4)) * 2 + lax.rem(core + dc, 2)
        pl.semaphore_signal(barrier, inc=1, device_id={"clip": there}, device_id_type=MESH)
    for d in range(1, TM):
        there = lax.rem(pos + d, TM)
        pl.semaphore_signal(barrier, inc=1, device_id={"tm": there}, device_id_type=MESH)

    for copy in small_copies[1:]:
        copy.start()
    w_copies = []
    for kt in range(3):
        for kw in range(3):
            for odd in range(2):
                copy = pltpu.make_async_copy(
                    w_hbm.at[kt, :, kw],
                    wide_w.at[kt * 3 + kw, pl.ds(odd, 3), :, pl.ds(odd * CHANS, CHANS)],
                    w_sem.at[(kt * 3 + kw) * 2 + odd],
                )
                copy.start()
                w_copies.append(copy)

    small_copies[0].wait()
    step_row = place_of(bucket_s[...])
    step_col = column_of(step_row)
    r = lax.broadcasted_iota(jnp.int32, (TILES, TILES), 0)
    c = lax.broadcasted_iota(jnp.int32, (TILES, TILES), 1)
    other = jnp.broadcast_to(step_row, (TILES, TILES))
    mine = jnp.broadcast_to(step_col, (TILES, TILES))
    ahead = jnp.where((other < mine) | ((other == mine) & (c < r)), 1, 0)
    place_col = jnp.sum(ahead, axis=1, keepdims=True)
    lanes = lax.broadcasted_iota(jnp.int32, (TILES, CHANS), 1)
    tiles_down = lax.broadcasted_iota(jnp.int32, (TILES, CHANS), 0)
    order = jnp.sum(jnp.where(place_col == lanes, tiles_down, 0), axis=0, keepdims=True)
    start = jnp.sum(jnp.where(step_col < lanes, 1, 0), axis=0, keepdims=True)
    table_v[...] = jnp.zeros_like(table_v)
    table_v[0:1, :] = order
    table_v[1:2, :] = start
    table_copy = pltpu.make_async_copy(table_v, table, local_sem.at[1])
    table_copy.start()

    zeros_w = jnp.zeros((9, CHANS, CHANS), jnp.bfloat16)
    wide_w[:, 3, :, 0:CHANS] = zeros_w
    wide_w[:, 0, :, CHANS : 2 * CHANS] = zeros_w
    pad = jnp.zeros((6, 16, CHANS), jnp.bfloat16)
    for kw in range(3):
        acts[kw, 0, :, 0] = pad
        acts[kw, 1, :, 4] = pad

    def raw_copy(j):
        return pltpu.make_async_remote_copy(
            src_ref=raw_out.at[j],
            dst_ref=raw_in.at[j],
            send_sem=raw_ssem.at[j],
            recv_sem=raw_rsem.at[j],
            device_id={"clip": target(j)},
            device_id_type=MESH,
        )

    def early_slots(j):
        first, after = table[1, CLIP - EARLY + j], table[1, CLIP - EARLY + 1 + j]
        places = [first, first + 1]
        return [(table[0, jnp.minimum(at, TILES - 1)], after > at) for at in places]

    table_copy.wait()
    for copy in x_copies:
        copy.wait()

    pl.semaphore_wait(barrier, CLIP - 1 + TM - 1)

    @pl.loop(0, EARLY)
    def _(j):
        for i, (t, _) in enumerate(early_slots(j)):
            raw_out[j, i] = x_s[t]
        raw_copy(j).start()

    def stat_copy(d, there):
        return pltpu.make_async_remote_copy(
            src_ref=stats.at[pos],
            dst_ref=stats.at[there],
            send_sem=stat_ssem.at[d],
            recv_sem=stat_rsem.at[d],
            device_id={"tm": lax.rem(pos + d, TM)},
            device_id_type=MESH,
        )

    for q in range(CHUNKS):
        @pl.loop(q * (TILES // CHUNKS), (q + 1) * (TILES // CHUNKS), unroll=4)
        def _(t):
            xf = x_s[t].astype(jnp.float32)
            pivot = xf[0:1]
            dev = (xf - pivot).reshape(ROWS // 8, 8, CHANS)
            first = jnp.sum(jnp.sum(dev, axis=0), axis=0, keepdims=True) * (1.0 / ROWS)
            second = jnp.sum(jnp.sum(dev * dev, axis=0), axis=0, keepdims=True)
            stats[pos, 0, pl.ds(t, 1), :] = pivot + first
            stats[pos, 1, pl.ds(t, 1), :] = jnp.maximum(second - float(ROWS) * (first * first), 0.0)

    for d in range(1, TM):
        stat_copy(d, pos).start()

    def halo_copy(m):
        return pltpu.make_async_remote_copy(
            src_ref=halo_out.at[m],
            dst_ref=halo_in.at[m],
            send_sem=halo_ssem.at[m],
            recv_sem=halo_rsem.at[m],
            device_id={"tm": lax.rem(pos + 1, TM)},
            device_id_type=MESH,
        )

    @pl.loop(0, PAIRS)
    def _(m):
        for i in range(2):
            halo_out[m, i] = x_s[table[0, 2 * m + i], ROWS // 2 : ROWS, :]

        @pl.when(pos < TM - 1)
        def _():
            halo_copy(m).start()


    for copy in small_copies[1:]:
        copy.wait()
    for d in range(1, TM):
        stat_copy(d, lax.rem(pos + TM - d, TM)).wait_recv()

    length = column_of(frames_row[...])
    total = jnp.zeros((TILES, CHANS), jnp.float32)
    weights = [jnp.where(length > 4 * j, 1.0, 0.0) for j in range(TM)]
    parts = weights[0] + weights[1] + weights[2] + weights[3]
    for j in range(TM):
        total = total + stats[j, 0] * weights[j]
    mean = group_sum(total) / (parts * 4.0)
    spread = jnp.zeros((TILES, CHANS), jnp.float32)
    for j in range(TM):
        dev = stats[j, 0] - mean
        spread = spread + (stats[j, 1] + float(ROWS) * (dev * dev)) * weights[j]
    var = group_sum(spread) / (parts * (4.0 * ROWS))
    mean_s[...] = mean
    scale_s[...] = lax.rsqrt(var + 1e-06) * (0.5 * gain_ref[...])

    half_shift = 0.5 * shift_ref[...]
    bias = bias_ref[...]
    for copy in w_copies:
        copy.wait()

    def fill(i, slot, at, held):
        got = done[jnp.minimum(at, TILES - 1)]
        send[i, slot] = jnp.where(held, got, jnp.zeros_like(got))

    def out_copy(i):
        return pltpu.make_async_remote_copy(
            src_ref=send.at[i],
            dst_ref=out_ref.at[me],
            send_sem=out_ssem.at[i],
            recv_sem=out_rsem.at[i],
            device_id={"clip": target(i + EARLY)},
            device_id_type=MESH,
        )

    def fill_both(i):
        first, after = table[1, i], table[1, i + 1]
        fill(i, 0, first, after > first)
        fill(i, 1, first + 1, after > first + 1)

    def unit(tiles):
        series = []
        for cells, before, mean_t, scale_t in tiles:
            xb = cells.astype(jnp.float32).reshape(4, 8, 8, CHANS)
            hb = before.astype(jnp.float32).reshape(2, 8, 8, CHANS)
            hb = jnp.where(pos == 0, jnp.broadcast_to(xb[0:1], hb.shape), hb)
            raw = jnp.concatenate([hb, xb], axis=0)
            mean_t = mean_t.reshape(1, 1, 1, CHANS)
            scale_t = scale_t.reshape(1, 1, 1, CHANS)
            h = (raw - mean_t) * scale_t + half_shift.reshape(1, 1, 1, CHANS)
            series.append((h * jnp.tanh(h) + h).reshape(48, 8, CHANS))
        w = lax.broadcasted_iota(jnp.int32, (48, 8, CHANS), 1)
        for kw in range(3):
            moved = []
            for act in series:
                if kw == 0:
                    act = jnp.where(w == 0, 0.0, pltpu.roll(act, 1, 1))
                if kw == 2:
                    act = jnp.where(w == 7, 0.0, pltpu.roll(act, 7, 1))
                moved.append(act.reshape(6, 8, 1, 8, CHANS))
            both = jnp.concatenate(moved, axis=2).reshape(6, 4, 2, 16, CHANS).astype(jnp.bfloat16)
            acts[kw, 1, :, 0:4] = both[:, :, 0]
            acts[kw, 0, :, 1:5] = both[:, :, 1]
        cols = []
        for kt in range(3):
            for kw in range(3):
                for j in range(4):
                    part = acts[kw, j % 2, kt : kt + 4, j // 2 : j // 2 + 4]
                    cols.append(part.reshape(256, CHANS))
        conv = jnp.dot(
            jnp.concatenate(cols, axis=1),
            wide_w[...].reshape(36 * CHANS, 2 * CHANS),
            preferred_element_type=jnp.float32,
        )
        rows = [
            conv[:, 0:CHANS].reshape(4, 4, 2, 8, CHANS),
            conv[:, CHANS:].reshape(4, 4, 2, 8, CHANS),
        ]
        results = []
        for i, (cells, _, _, _) in enumerate(tiles):
            both = jnp.concatenate([v[:, :, i : i + 1] for v in rows], axis=2)
            results.append(cells.astype(jnp.float32) + both.reshape(ROWS, CHANS) + bias)
        return results

    def late_copy(j):
        return pltpu.make_async_remote_copy(
            src_ref=raw_in.at[j, :, pl.ds(ROWS // 2, ROWS // 2)],
            dst_ref=late_halo.at[j],
            send_sem=late_ssem.at[j],
            recv_sem=late_rsem.at[j],
            device_id={"tm": lax.rem(pos + 1, TM)},
            device_id_type=MESH,
        )

    def notes_copy(j):
        return pltpu.make_async_remote_copy(
            src_ref=notes_out.at[j],
            dst_ref=notes_in.at[j],
            send_sem=notes_ssem.at[j],
            recv_sem=notes_rsem.at[j],
            device_id={"clip": target(j)},
            device_id_type=MESH,
        )

    @pl.loop(0, EARLY)
    def _(j):
        notes_out[j] = jnp.zeros((8, CHANS), jnp.float32)
        for i, (t, held) in enumerate(early_slots(j)):
            notes_out[j, i : i + 1] = mean_s[pl.ds(t, 1), :]
            notes_out[j, 2 + i : 3 + i] = scale_s[pl.ds(t, 1), :]
            valid = held & (frames_smem[t] > 4 * pos)
            notes_out[j, 4 + i : 5 + i] = jnp.where(valid, jnp.ones((1, CHANS)), jnp.zeros((1, CHANS)))
        notes_copy(j).start()

    @pl.loop(0, PAIRS)
    def _(m):

        @pl.when(pos > 0)
        def _():
            halo_copy(m).wait_recv()

        tiles = [table[0, 2 * m + i] for i in range(2)]
        results = unit(
            [
                (x_s[t], halo_in[m, i], mean_s[pl.ds(t, 1), :], scale_s[pl.ds(t, 1), :])
                for i, t in enumerate(tiles)
            ]
        )
        for i, t in enumerate(tiles):
            valid = frames_smem[t] > 4 * pos
            res = results[i]
            done[2 * m + i] = jnp.where(valid, res, jnp.zeros_like(res)).astype(jnp.bfloat16)
        fill_both(m)
        out_copy(m).start()

        @pl.when(m >= PAIRS - EARLY)
        def _():
            raw_copy(m - (PAIRS - EARLY)).wait_recv()

            @pl.when(pos < TM - 1)
            def _():
                late_copy(m - (PAIRS - EARLY)).start()


    @pl.loop(PAIRS, SENDS)
    def _(i):
        fill_both(i)
        out_copy(i).start()

    fill_both(SENDS)
    own = pltpu.make_async_copy(send.at[SENDS], out_ref.at[me], local_sem.at[2])
    own.start()

    def late_out(j):
        return pltpu.make_async_copy(late_done.at[j], out_ref.at[origin(j)], late_sem.at[j])

    @pl.loop(0, EARLY)
    def _(j):

        @pl.when(pos > 0)
        def _():
            late_copy(j).wait_recv()

        notes_copy(j).wait_recv()
        results = unit(
            [
                (raw_in[j, i], late_halo[j, i], notes_in[j, i : i + 1], notes_in[j, 2 + i : 3 + i])
                for i in range(2)
            ]
        )
        for i in range(2):
            valid = notes_in[j, 4 + i : 5 + i] > 0.5
            res = results[i]
            late_done[j, i] = jnp.where(valid, res, jnp.zeros_like(res)).astype(jnp.bfloat16)
        late_out(j).start()

    for d in range(1, TM):
        stat_copy(d, pos).wait_send()

    @pl.loop(0, PAIRS)
    def _(m):

        @pl.when(pos < TM - 1)
        def _():
            halo_copy(m).wait_send()


    @pl.loop(0, EARLY)
    def _(j):
        raw_copy(j).wait_send()

        @pl.when(pos < TM - 1)
        def _():
            late_copy(j).wait_send()

        notes_copy(j).wait_send()
        late_out(j).wait()

    own.wait()

    @pl.loop(0, SENDS)
    def _(i):
        out_copy(i).wait_send()

    @pl.loop(0, SENDS)
    def _(i):
        out_copy(i).wait_recv()


def on_device(tiles, buckets, tile_frames, norm_gain, norm_shift, conv_weight, conv_bias):
    hbm = pl.BlockSpec(memory_space=pltpu.HBM)
    any_ = pl.BlockSpec(memory_space=pl.ANY)
    bf16, f32 = jnp.bfloat16, jnp.float32
    out = pl.pallas_call(
        kernel,
        out_shape=jax.ShapeDtypeStruct((CLIP, 2, ROWS, CHANS), bf16),
        in_specs=[hbm] * 8,
        out_specs=any_,
        scratch_shapes=[
            pltpu.VMEM((TILES, ROWS, CHANS), bf16),
            pltpu.VMEM((1, TILES), jnp.int32),
            pltpu.VMEM((1, TILES), jnp.int32),
            pltpu.SMEM((TILES,), jnp.int32),
            pltpu.VMEM((1, CHANS), f32),
            pltpu.VMEM((1, CHANS), f32),
            pltpu.VMEM((1, CHANS), f32),
            pltpu.VMEM((PAIRS, 2, ROWS // 2, CHANS), bf16),
            pltpu.VMEM((PAIRS, 2, ROWS // 2, CHANS), bf16),
            pltpu.VMEM((TM, 2, TILES, CHANS), f32),
            pltpu.VMEM((TILES, CHANS), f32),
            pltpu.VMEM((TILES, CHANS), f32),
            pltpu.VMEM((3, 2, 6, 5, 16, CHANS), bf16),
            pltpu.VMEM((9, 4, CHANS, 2 * CHANS), bf16),
            pltpu.VMEM((TILES, ROWS, CHANS), bf16),
            pltpu.VMEM((SENDS + 1, 2, ROWS, CHANS), bf16),
            pltpu.VMEM((8, CHANS), jnp.int32),
            pltpu.SMEM((8, CHANS), jnp.int32),
            pltpu.VMEM((EARLY, 2, ROWS, CHANS), bf16),
            pltpu.VMEM((EARLY, 2, ROWS, CHANS), bf16),
            pltpu.VMEM((EARLY, 2, ROWS // 2, CHANS), bf16),
            pltpu.VMEM((EARLY, 2, ROWS, CHANS), bf16),
            pltpu.VMEM((EARLY, 8, CHANS), f32),
            pltpu.VMEM((EARLY, 8, CHANS), f32),
            pltpu.SemaphoreType.DMA((CHUNKS,)),
            pltpu.SemaphoreType.DMA((6,)),
            pltpu.SemaphoreType.DMA((18,)),
            pltpu.SemaphoreType.DMA((3,)),
            pltpu.SemaphoreType.DMA((PAIRS,)),
            pltpu.SemaphoreType.DMA((PAIRS,)),
            pltpu.SemaphoreType.DMA((TM,)),
            pltpu.SemaphoreType.DMA((TM,)),
            pltpu.SemaphoreType.DMA((SENDS,)),
            pltpu.SemaphoreType.DMA((SENDS,)),
            pltpu.SemaphoreType.DMA((EARLY,)),
            pltpu.SemaphoreType.DMA((EARLY,)),
            pltpu.SemaphoreType.DMA((EARLY,)),
            pltpu.SemaphoreType.DMA((EARLY,)),
            pltpu.SemaphoreType.DMA((EARLY,)),
            pltpu.SemaphoreType.DMA((EARLY,)),
            pltpu.SemaphoreType.DMA((EARLY,)),
        ],
        compiler_params=pltpu.CompilerParams(
            collective_id=0, has_side_effects=True, vmem_limit_bytes=40 << 20
        ),
        name="encode_and_send",
    )(
        *[
            pltpu.with_memory_space_constraint(v, pltpu.HBM)
            for v in (
                tiles.reshape(TILES, ROWS, CHANS),
                buckets.reshape(1, TILES),
                tile_frames.reshape(1, TILES),
                tile_frames,
                norm_gain.reshape(1, CHANS),
                norm_shift.reshape(1, CHANS),
                conv_weight,
                conv_bias.reshape(1, CHANS),
            )
        ]
    )
    return out.reshape((2 * CLIP,) + tiles.shape[1:])


def solution(mesh):
    in_specs = (P("clip", "tm", None, None, None), P("clip", None), P("clip"), P(), P(), P(), P())
    out_specs = P("clip", "tm", None, None, None)
    return jax.shard_map(
        on_device, mesh=mesh, in_specs=in_specs, out_specs=out_specs, check_vma=False
    )
```
